32 devices in a mesh: cache: 8 (over y, x, core), batch: 4 (over z).
Axes of the slice: x: 2, y: 2, z: 4, core: 2. Of those that a mesh axis runs over, the one named last changes fastest.
Arguments:
- queries: bfloat16 [3, 4096, 768], P(None, 'batch')
- positives: int32 [3, 4096], P(None, 'batch'), may hold values from 0 to 511
- block_list: int32 [3, 32, 48], P(None, 'batch'), may hold values from 0 to 63
- block_count: int32 [3, 32], P(None, 'batch'), may hold values from 1 to 48
- refresh_owner: int32 [3], replicated, may hold values from 0 to 7, as said below
- cache: float32 [8192, 768], P('cache'), may hold values from -6 to 6
- fresh: float32 [4096, 768], P('cache')
Outputs:
- query_grad: float32 [3, 4096, 768], P(None, ('batch', 'cache'))
- cache_grad: float32 [8192, 768], P('cache')
The draws below stay inside these ranges and needn't reach their ends.
Inputs may be any that keep to these rules, and one draw needn't show every extreme that they name: `refresh_owner`: 3 different owners; owner 0 and owner 8 - 1 are always among them.
All inputs are finite; a program needn't handle non-finite values.
Results may differ from the reference program's by a relative error of at most 0.0003.
Values sent between devices are 32-bit elements; how exact they have to be, the bound alone decides.
No kernel may reach another device: no remote copies, remote signals or barrier semaphores. Data moves between devices by JAX's collectives and lax.ppermute only.
A program may use at most 128 MiB of HBM per device.

```python
import math
import jax
import jax.numpy as jnp
from jax import lax

D = 768
BLK = 128
CACHE_DEV = 1024
STEPS = 3
SLAB = 512
OWNERS = 8
QUERIES = 4096
QUERY_BLOCKS = 32
BLOCKS = 64
MAXL = 48
N_CACHE = 8


def owner_order(key):
    base_key = jax.random.fold_in(key, 5)
    first_key, second_key = jax.random.split(base_key)
    middle = 1 + jax.random.permutation(first_key, OWNERS - 2)[:STEPS - 2].astype(jnp.int32)
    chosen = jnp.concatenate([jnp.array([0, OWNERS - 1], jnp.int32), middle], axis=0)
    order = jax.random.permutation(second_key, STEPS)
    return jnp.take(chosen, order, axis=0).astype(jnp.int32)


def fresh_values(key):
    base_key = jax.random.fold_in(key, 11)
    return jax.random.normal(base_key, (SLAB * OWNERS, D), jnp.float32)


def draw_refresh_owner(key, part):
    return owner_order(key)


def draw_fresh(key, part):
    return fresh_values(key)


def draw_queries(key, part):
    own_key = jax.random.fold_in(key, 17)
    return jax.random.normal(own_key, (STEPS, QUERIES, D), jnp.float32).astype(jnp.bfloat16)


def draw_block_count(key, part):
    count_key = jax.random.fold_in(key, 23)
    first_key, second_key, third_key = jax.random.split(count_key, 3)
    total = STEPS * QUERY_BLOCKS
    counts = jax.random.randint(first_key, (total,), 1, MAXL + 1, jnp.int32)
    high_slot = jax.random.randint(second_key, (), 0, total, jnp.int32)
    low_slot = (high_slot + 1 + jax.random.randint(third_key, (), 0, total - 1, jnp.int32)) % total
    counts = counts.at[high_slot].set(MAXL).at[low_slot].set(1)
    return counts.reshape(STEPS, QUERY_BLOCKS)


def touch_ends(values, key, smallest, top_value):
    extent = values.shape
    place = [jax.random.randint(jax.random.fold_in(key, axis), (), 0, extent[axis]) for axis in range(len(extent))]
    values = values.at[tuple(place)].set(smallest)
    longest = extent.index(max(extent))
    place[longest] = (place[longest] + 1) % extent[longest]
    return values.at[tuple(place)].set(top_value)


def block_levels(key, dims, cuts, low, top_value):
    factor_of = 1.0
    for position, blocks in cuts:
        heights = jax.random.uniform(jax.random.fold_in(jax.random.fold_in(key, 6), position), (blocks,), jnp.float32, low / len(cuts), top_value / len(cuts))
        factor_of = factor_of * jnp.repeat(jnp.exp(heights), dims[position] // blocks).reshape((-1,) + (1,) * (len(dims) - 1 - position))
    return factor_of


def centred(stream_key, extent, deviation, most, pieces=(), kind=jnp.bfloat16):
    values = deviation * jax.random.normal(stream_key, extent, jnp.float32)
    if pieces:
        values = values * block_levels(stream_key, extent, pieces, -0.22, 0.18)
    return jnp.clip(values, -most, most).astype(kind)


def setup_inputs(seed: int = 0) -> dict:
    streams_of = jax.random.split(jax.random.key(seed), 8)
    queries = draw_queries(jax.random.fold_in(streams_of[7], 71), 0)
    positives = touch_ends(jax.random.randint(streams_of[1], (STEPS, QUERIES), 0, SLAB), jax.random.fold_in(streams_of[1], 1), 0, SLAB - 1).astype(jnp.int32)
    block_list = touch_ends(jax.random.randint(streams_of[2], (STEPS, QUERY_BLOCKS, MAXL), 0, BLOCKS), jax.random.fold_in(streams_of[2], 1), 0, BLOCKS - 1).astype(jnp.int32)
    block_count = draw_block_count(jax.random.fold_in(streams_of[7], 71), 0)
    refresh_owner = draw_refresh_owner(jax.random.fold_in(streams_of[7], 71), 0)
    cache = centred(streams_of[5], (CACHE_DEV * N_CACHE, D), 1.0, 6.0, ((0, 8),), jnp.float32)
    fresh = draw_fresh(jax.random.fold_in(streams_of[7], 71), 0)
    return dict(queries=queries, positives=positives, block_list=block_list, block_count=block_count, refresh_owner=refresh_owner, cache=cache, fresh=fresh)


def reference(queries, positives, block_list, block_count, refresh_owner, cache, fresh):
    scale = 2.0 / math.sqrt(D)
    highest = lax.Precision.HIGHEST
    current = cache
    grad_cache = jnp.zeros(cache.shape, jnp.float32)
    results = []
    block_ids = jnp.arange(BLOCKS, dtype=jnp.int32)
    for step in range(STEPS):
        owner = refresh_owner[step].astype(jnp.int32)
        slab = lax.dynamic_slice_in_dim(fresh, owner * SLAB, SLAB, 0)
        current = lax.dynamic_update_slice_in_dim(current, slab, owner * CACHE_DEV, 0)
        valid = jnp.arange(MAXL, dtype=jnp.int32)[None, :] < block_count[step][:, None]
        hits = (block_list[step][:, :, None] == block_ids[None, None, :]) & valid[:, :, None]
        member = jnp.any(hits, axis=1)
        query_rows = queries[step].astype(jnp.float32).reshape(QUERY_BLOCKS, BLK, D)
        pos_rows = positives[step].reshape(QUERY_BLOCKS, BLK)

        def per_block(carry, item):
            block_q, block_member, block_pos = item
            mask = jnp.repeat(block_member, BLK)
            scores = scale * jnp.dot(block_q, current.T, precision=highest)
            scores = jnp.where(mask[None, :], scores, -1e+30)
            slab_scores = scale * jnp.dot(block_q, slab.T, precision=highest)
            top = jnp.maximum(lax.optimization_barrier(jnp.max(scores, axis=1)), lax.optimization_barrier(jnp.max(slab_scores, axis=1)))
            total = lax.optimization_barrier(jnp.sum(jnp.where(mask[None, :], jnp.exp(scores - top[:, None]), 0.0), axis=1))
            total = total + lax.optimization_barrier(jnp.sum(jnp.exp(slab_scores - top[:, None]), axis=1))
            lse = top + jnp.log(total)
            probs = jnp.where(mask[None, :], jnp.exp(scores - lse[:, None]), 0.0)
            slab_probs = jnp.exp(slab_scores - lse[:, None])
            grad_q = jnp.dot(probs, current, precision=highest) + jnp.dot(slab_probs, slab, precision=highest)
            grad_q = grad_q - jnp.take(slab, block_pos, axis=0)
            carry = carry + jnp.dot(probs.T, block_q, precision=highest)
            return (carry, grad_q)
        grad_cache, grads = lax.scan(per_block, grad_cache, (query_rows, member, pos_rows))
        results.append(grads.reshape(QUERIES, D))
    return (jnp.stack(results, axis=0), grad_cache)
```

```python
import math

import jax
import jax.numpy as jnp
from jax import lax
from jax.sharding import PartitionSpec as P

BLK = 128
LOW = -1e30


def split(x):
    hi = lax.reduce_precision(x, exponent_bits=8, mantissa_bits=7)
    return hi.astype(jnp.bfloat16), (x - hi).astype(jnp.bfloat16)


def mm(a, b, ca, cb):
    return lax.dot_general(a, b, (((ca,), (cb,)), ((), ())), preferred_element_type=jnp.float32)


def swap(x, axis, bit):
    n = lax.axis_size(axis)
    return lax.ppermute(x, axis, [(i, i ^ bit) for i in range(n)])


def exchange_lse(lse):
    n = lax.axis_size("cache")
    bit = 1
    while bit < n:
        lse = jnp.logaddexp(lse, swap(lse, "cache", bit))
        bit *= 2
    return lse


def reduce_home(parts):
    n = len(parts)
    got = swap(jnp.stack(parts[1::2]), "cache", 1)
    held = {r: parts[r] + got[r // 2] for r in range(0, n, 2)}
    half = parts[0].shape[1] // 2
    bits = [b for b in (2, 4, 8, 16, 32, 64) if b < n]
    out = []
    for lo, order in ((0, bits), (half, bits[::-1])):
        cur = {r: held[r][:, lo:lo + half] for r in held}
        for bit in order:
            away = [r for r in sorted(cur) if r & bit]
            got = swap(jnp.stack([cur[r] for r in away]), "cache", bit)
            cur = {r ^ bit: cur[r ^ bit] + got[i] for i, r in enumerate(away)}
        out.append(cur[0])
    return jnp.concatenate(out, axis=1)


def sum_line(chunks):
    n = lax.axis_size("batch")
    if n != 4:
        return [lax.psum(c, "batch") for c in chunks]
    at = lax.axis_index("batch")
    end = (at == 0) | (at == 3)
    out = []
    for c in chunks:
        inner = c + lax.ppermute(c, "batch", [(0, 1), (3, 2)])
        total = inner + lax.ppermute(inner, "batch", [(1, 2), (2, 1)])
        out.append(jnp.where(end, lax.ppermute(total, "batch", [(1, 0), (2, 3)]), total))
    return out


def on_device(queries, positives, block_list, block_count, refresh_owner, cache, fresh):
    steps, group_rows, width = queries.shape
    cache_rows = cache.shape[0]
    slab_rows = fresh.shape[0]
    owners = lax.axis_size("cache")
    me = lax.axis_index("cache")
    share = group_rows // owners
    list_width = block_list.shape[2]
    own_blocks = cache_rows // BLK
    scale = 2.0 / math.sqrt(width)
    block_ids = me * own_blocks + jnp.arange(own_blocks, dtype=jnp.int32)
    valid = jnp.arange(list_width, dtype=jnp.int32)[None, None, :] < block_count[:, :, None]
    hits = (block_list[..., None] == block_ids) & valid[..., None]
    member = jnp.any(hits, axis=2)
    is_owner = refresh_owner == me
    is_slab = jnp.arange(own_blocks) < slab_rows // BLK
    weight = member.astype(jnp.float32) + (is_owner[:, None, None] & is_slab).astype(jnp.float32)

    def spread(x):
        return jnp.repeat(jnp.repeat(x, BLK, axis=0), BLK, axis=1)

    scores, lses, currents = [], [], []
    current = cache
    for s in range(steps):
        current = jnp.where(is_owner[s], jnp.concatenate([fresh, current[slab_rows:]], axis=0), current)
        hi, lo = split(current)
        currents.append((hi, lo))
        z = scale * (mm(queries[s], hi, 1, 1) + mm(queries[s], lo, 1, 1))
        w = spread(weight[s])
        z = jnp.where(w > 0, z, LOW)
        top = jnp.max(z, axis=1)
        total = jnp.sum(w * jnp.exp(z - top[:, None]), axis=1)
        scores.append(z)
        lses.append(jnp.where(total > 0, top + jnp.log(jnp.maximum(total, 1e-30)), LOW))
    lse = exchange_lse(jnp.stack(lses))
    grad = jnp.zeros((cache_rows, width), jnp.float32)
    terms = []
    for s in range(steps):
        p = jnp.exp(scores[s] - lse[s][:, None])
        hi, lo = split(jnp.where(spread(member[s]), p, 0.0))
        grad = grad + mm(hi, queries[s], 0, 0) + mm(lo, queries[s], 0, 0)
        hot = (positives[s][:, None] == jnp.arange(cache_rows)[None, :]) & is_owner[s]
        hi, lo = split(spread(weight[s]) * p - hot.astype(jnp.float32))
        chi, clo = currents[s]
        terms.append(mm(hi, chi, 1, 0) + mm(lo, chi, 1, 0) + mm(hi, clo, 1, 0))
    term = jnp.stack(terms)
    chunks = sum_line([grad[i:i + BLK] for i in range(0, cache_rows, BLK)])
    parts = [lax.dynamic_slice_in_dim(term, (me ^ r) * share, share, 1) for r in range(owners)]
    mine = reduce_home(parts)
    return mine, jnp.concatenate(chunks, axis=0)


def solution(mesh):
    return jax.shard_map(
        on_device,
        mesh=mesh,
        in_specs=(
            P(None, "batch", None),
            P(None, "batch"),
            P(None, "batch", None),
            P(None, "batch"),
            P(),
            P("cache", None),
            P("cache", None),
        ),
        out_specs=(P(None, ("batch", "cache"), None), P("cache", None)),
        check_vma=False,
    )
```

```python
import functools
import math

import jax
import jax.numpy as jnp
from jax import lax
from jax.experimental import pallas as pl
from jax.experimental.pallas import tpu as pltpu
from jax.sharding import PartitionSpec as P

BLK = 128
LOW = -1e30
VMEM_BYTES = 56 * 1024 * 1024


def dot(a, b, ca, cb):
    return lax.dot_general(a, b, (((ca,), (cb,)), ((), ())), preferred_element_type=jnp.float32)


def split(x):
    hi = x.astype(jnp.bfloat16)
    return hi, (x - hi.astype(jnp.float32)).astype(jnp.bfloat16)


def as_columns(row):
    return jnp.broadcast_to(row, (BLK, row.shape[1])).T


class Meta:
    def __init__(self, steps, groups, blocks, slab_blocks):
        self.steps, self.groups, self.blocks, self.slab_blocks = steps, groups, blocks, slab_blocks
        self.size = steps * groups * blocks

    def count(self, ref, s, b, j):
        return ref[(s * self.groups + b) * self.blocks + j]

    def member(self, ref, sb, j):
        return ref[self.size + sb * self.blocks + j]

    def own(self, ref, s):
        return ref[2 * self.size + s]

    def replaced(self, ref, s):
        return ref[2 * self.size + self.steps + s]

    def source(self, ref, s, j):
        return jnp.where((self.replaced(ref, s) > 0) & (j < self.slab_blocks), self.blocks + j, j)


def scores_kernel(meta, part, scale, info, q_ref, cache_ref, fresh_ref, z_ref, lse_ref, w_out, w_ref, mx, sem):
    i = pl.program_id(0)
    per = meta.groups // part
    s, first = i // per, (i % per) * part

    @pl.when(i == 0)
    def _():
        for src, at, n in ((cache_ref, 0, meta.blocks), (fresh_ref, meta.blocks, meta.slab_blocks)):
            def one(k, _, src=src, at=at):
                hi, lo = split(src[pl.ds(pl.multiple_of(k * BLK, BLK), BLK), :])
                w_ref[at + k, :BLK] = hi
                w_ref[at + k, BLK:] = lo
                return 0
            lax.fori_loop(0, n, one, 0)
        pltpu.make_async_copy(w_ref, w_out, sem).start()

    def block(j, _):
        both = dot(q_ref[0], w_ref[meta.source(info, s, j)], 1, 1)
        z = (both[:, :BLK] + both[:, BLK:]) * scale
        for b in range(part):
            zb = z[b * BLK:(b + 1) * BLK]
            z_ref[0, b, j] = zb
            zb = jnp.where(meta.count(info, s, first + b, j) > 0, zb, LOW)
            mx[b] = jnp.where(j > 0, jnp.maximum(mx[b], zb), zb)
        return 0

    lax.fori_loop(0, meta.blocks, block, 0)
    for b in range(part):
        top = jnp.max(mx[b], axis=1, keepdims=True)
        acc = jnp.zeros((BLK, BLK), jnp.float32)
        for j in range(meta.blocks):
            c = meta.count(info, s, first + b, j)
            acc += jnp.where(c > 0, jnp.exp(z_ref[0, b, j] - top), 0.0) * c.astype(jnp.float32)
        total = jnp.sum(acc, axis=1, keepdims=True)
        lse = jnp.where(total > 0, top + jnp.log(jnp.maximum(total, 1e-30)), LOW)
        lse_ref[0, b:b + 1, :] = jnp.broadcast_to(lse, (BLK, BLK)).T[:1]

    @pl.when(i == pl.num_programs(0) - 1)
    def _():
        pltpu.make_async_copy(w_ref, w_out, sem).wait()


def grad_kernel(meta, first, width, info, z_ref, q_ref, lse_ref, dep, out_ref, tok_ref, todo):
    j = first + pl.program_id(0)
    total = meta.steps * meta.groups

    def collect(sb, n):
        todo[n] = sb
        return n + meta.member(info, sb, j)

    n = lax.fori_loop(0, total, collect, 0)
    for g in range(width):
        todo[n + g] = 0
    out_ref[...] = jnp.zeros_like(out_ref)
    tok_ref[...] = jnp.zeros_like(tok_ref)

    def step(it, _):
        his, los, rows = [], [], []
        for g in range(width):
            k = it * width + g
            sb = todo[k]
            p = jnp.exp(z_ref[sb, 0].T - lse_ref[pl.ds(sb, 1), :])
            hi, lo = split(jnp.where(k < n, p, 0.0))
            his.append(hi)
            los.append(lo)
            rows.append(q_ref[sb])
        left = jnp.concatenate([jnp.concatenate(his, axis=1), jnp.concatenate(los, axis=1)], axis=0)
        acc = dot(left, jnp.concatenate(rows, axis=0), 1, 0)
        out_ref[...] += acc[:BLK] + acc[BLK:]
        return 0

    lax.fori_loop(0, (n + width - 1) // width, step, 0)


def term_kernel(meta, first, width, info, z_ref, w_ref, lse_ref, pos_ref, dep, old, out_ref, tok_ref, todo):
    b = first + pl.program_id(0)
    tok_ref[...] = jnp.zeros_like(tok_ref)
    lane = lax.broadcasted_iota(jnp.int32, (BLK, BLK), 1).astype(jnp.float32)

    def one_step(s, _):
        lse = as_columns(lse_ref[s, pl.ds(b, 1), :])
        pos = as_columns(pos_ref[s, pl.ds(b, 1), :]) - lane
        own = meta.own(info, s)

        def collect(j, n):
            todo[n] = j
            return n + (meta.count(info, s, b, j) > 0).astype(jnp.int32)

        n = lax.fori_loop(0, meta.blocks, collect, 0)
        for g in range(width):
            todo[n + g] = 0
        out_ref[0, s] = jnp.zeros(out_ref.shape[2:], jnp.float32)

        def step(it, _):
            his, los, chi, clo = [], [], [], []
            for g in range(width):
                k = it * width + g
                j = todo[k]
                p = jnp.exp(z_ref[s, 0, j] - lse) * meta.count(info, s, b, j).astype(jnp.float32)
                hot = (own > 0) & (j < meta.slab_blocks)
                p = p - jnp.where(pos == (j * BLK).astype(jnp.float32), hot.astype(jnp.float32), 0.0)
                hi, lo = split(jnp.where(k < n, p, 0.0))
                his.append(hi)
                los.append(lo)
                blk = meta.source(info, s, j)
                chi.append(w_ref[blk, :BLK])
                clo.append(w_ref[blk, BLK:])
            hi = jnp.concatenate(his, axis=1)
            acc = dot(jnp.concatenate([hi, jnp.concatenate(los, axis=1)], axis=0), jnp.concatenate(chi, axis=0), 1, 0)
            low = dot(hi, jnp.concatenate(clo, axis=0), 1, 0)
            out_ref[0, s] += acc[:BLK] + acc[BLK:] + low
            return 0

        lax.fori_loop(0, (n + width - 1) // width, step, 0)
        return 0

    lax.fori_loop(0, meta.steps, one_step, 0)


def params():
    return pltpu.CompilerParams(vmem_limit_bytes=VMEM_BYTES, dimension_semantics=("arbitrary",))


def whole(shape):
    return pl.BlockSpec(shape, lambda i, info: (0,) * len(shape))


def run_scores(meta, info, queries, cache, fresh):
    steps, rows, width = queries.shape
    part = min(4, meta.groups)
    per = meta.groups // part
    n_src = meta.blocks + meta.slab_blocks
    tok = (steps * meta.groups * meta.blocks) * BLK * BLK
    z, lse, w = pl.pallas_call(
        functools.partial(scores_kernel, meta, part, 2.0 / math.sqrt(width)),
        grid_spec=pltpu.PrefetchScalarGridSpec(
            num_scalar_prefetch=1,
            grid=(steps * per,),
            in_specs=[
                pl.BlockSpec((1, part * BLK, width), lambda i, info: (i // per, i % per, 0)),
                whole(cache.shape),
                whole(fresh.shape),
            ],
            out_specs=[
                pl.BlockSpec((1, part, meta.blocks, BLK, BLK), lambda i, info: (i // per, i % per, 0, 0, 0)),
                pl.BlockSpec((1, part, BLK), lambda i, info: (i, 0, 0)),
                pl.BlockSpec(memory_space=pl.ANY),
            ],
            scratch_shapes=[
                pltpu.VMEM((n_src, 2 * BLK, width), jnp.bfloat16),
                pltpu.VMEM((part, BLK, BLK), jnp.float32),
                pltpu.SemaphoreType.DMA,
            ],
        ),
        out_shape=[
            jax.ShapeDtypeStruct((steps, meta.groups, meta.blocks, BLK, BLK), jnp.float32),
            jax.ShapeDtypeStruct((steps * per, part, BLK), jnp.float32),
            jax.ShapeDtypeStruct((n_src, 2 * BLK, width), jnp.bfloat16),
        ],
        compiler_params=params(),
        cost_estimate=pl.CostEstimate(flops=4 * tok * width, bytes_accessed=30_000_000, transcendentals=tok),
        name="scores",
    )(info, queries, cache, fresh)
    return z, lse.reshape(steps, meta.groups, BLK), w


def run_grads(meta, info, z, queries, lse, first, count, dep):
    total = meta.steps * meta.groups
    width = queries.shape[-1]
    group = 4
    return pl.pallas_call(
        functools.partial(grad_kernel, meta, first, group),
        grid_spec=pltpu.PrefetchScalarGridSpec(
            num_scalar_prefetch=1,
            grid=(count,),
            in_specs=[
                pl.BlockSpec((total, 1, BLK, BLK), lambda i, info: (0, first + i, 0, 0)),
                whole((total, BLK, width)),
                whole((total, BLK)),
                pl.BlockSpec(memory_space=pl.ANY),
            ],
            out_specs=[pl.BlockSpec((BLK, width), lambda i, info: (i, 0)), whole((8, 128))],
            scratch_shapes=[pltpu.SMEM((total + group,), jnp.int32)],
        ),
        out_shape=[
            jax.ShapeDtypeStruct((count * BLK, width), jnp.float32),
            jax.ShapeDtypeStruct((8, 128), jnp.float32),
        ],
        compiler_params=params(),
        cost_estimate=pl.CostEstimate(
            flops=count * total * BLK * BLK * width * 2, bytes_accessed=count * 2_000_000 + 5_000_000, transcendentals=0),
        name="cache_grad",
    )(info, z.reshape(total, meta.blocks, BLK, BLK), queries.reshape(total, BLK, width), lse.reshape(total, BLK), dep)


def run_terms(meta, info, z, w, lse, pos, first, count, dep, old):
    width = w.shape[-1]
    group = 2
    shape = (meta.groups, meta.steps, BLK, width)
    aliased = old is not None
    return pl.pallas_call(
        functools.partial(term_kernel, meta, first, group),
        grid_spec=pltpu.PrefetchScalarGridSpec(
            num_scalar_prefetch=1,
            grid=(count,),
            in_specs=[
                pl.BlockSpec((meta.steps, 1, meta.blocks, BLK, BLK), lambda i, info: (0, first + i, 0, 0, 0)),
                whole(w.shape),
                whole(lse.shape),
                whole(pos.shape),
                pl.BlockSpec(memory_space=pl.ANY),
                pl.BlockSpec(memory_space=pl.ANY),
            ],
            out_specs=[
                pl.BlockSpec((1, meta.steps, BLK, width), lambda i, info: (first + i, 0, 0, 0)),
                whole((8, 128)),
            ],
            scratch_shapes=[pltpu.SMEM((meta.blocks + group,), jnp.int32)],
        ),
        out_shape=[jax.ShapeDtypeStruct(shape, jnp.float32), jax.ShapeDtypeStruct((8, 128), jnp.float32)],
        input_output_aliases={6: 0} if aliased else {},
        compiler_params=params(),
        cost_estimate=pl.CostEstimate(
            flops=count * meta.steps * meta.blocks * BLK * BLK * width * 3, bytes_accessed=count * 3_000_000 + 5_000_000,
            transcendentals=0),
        name="query_term",
    )(info, z, w, lse, pos, dep, old if aliased else dep)


def exchange_lse(lse):
    n = lax.axis_size("cache")
    bit = 1
    while bit < n:
        lse = jnp.logaddexp(lse, lax.ppermute(lse, "cache", [(i, i ^ bit) for i in range(n)]))
        bit *= 2
    return lse


def barrier(*values):
    return lax.optimization_barrier(tuple(values))


def sum_line(chunks, tok, jobs):
    if lax.axis_size("batch") != 4:
        out = [lax.psum(c, "batch") for c in chunks]
        for t in sorted(jobs):
            tok = jobs[t](tok)
        return out
    at = lax.axis_index("batch")
    end = (at == 0) | (at == 3)
    n, lag, ahead = len(chunks), 2, 3
    first, inner, second, total, third, out = {}, {}, {}, {}, {}, {}

    def send_in(k, value):
        first[k] = lax.ppermute(value, "batch", [(0, 1), (3, 2)])

    for k in range(ahead):
        send_in(k, chunks[k])
    prev = [tok]
    for t in range(n + 2 * lag):
        ops = []
        if t < n:
            ops += [chunks[t], first[t]]
        if 0 <= t - lag < n:
            ops += [inner[t - lag], second[t - lag]]
        if t >= 2 * lag:
            ops += [total[t - 2 * lag], third[t - 2 * lag]]
        if t - 1 in jobs:
            prev.append(jobs[t - 1](prev[0][:1, :1]))
        ops = list(barrier(*ops, *prev)[:len(ops)])
        new = []
        if t < n:
            new.append(ops[0] + ops[1])
            ops = ops[2:]
        if 0 <= t - lag < n:
            new.append(ops[0] + ops[1])
            ops = ops[2:]
        if t >= 2 * lag:
            new.append(jnp.where(end, ops[1], ops[0]))
        new = list(barrier(*new))
        prev = list(new)
        if t < n:
            inner[t] = new.pop(0)
            second[t] = lax.ppermute(inner[t], "batch", [(1, 2), (2, 1)])
        if 0 <= t - lag < n:
            total[t - lag] = new.pop(0)
            third[t - lag] = lax.ppermute(total[t - lag], "batch", [(1, 0), (2, 3)])
        if t >= 2 * lag:
            out[t - 2 * lag] = new.pop(0)
        if t + ahead < n:
            send_in(t + ahead, barrier(chunks[t + ahead], *prev)[0])
    return [out[k] for k in range(n)]


def on_device(queries, positives, block_list, block_count, refresh_owner, cache, fresh):
    steps, group_rows, width = queries.shape
    groups = group_rows // BLK
    blocks, slab_blocks = cache.shape[0] // BLK, fresh.shape[0] // BLK
    meta = Meta(steps, groups, blocks, slab_blocks)
    me = lax.axis_index("cache")
    block_ids = me * blocks + jnp.arange(blocks, dtype=jnp.int32)
    valid = jnp.arange(block_list.shape[2], dtype=jnp.int32)[None, None, :] < block_count[:, :, None]
    member = jnp.any((block_list[..., None] == block_ids) & valid[..., None], axis=2)
    own = refresh_owner == me
    counts = member.astype(jnp.int32) + (own[:, None, None] & (jnp.arange(blocks) < slab_blocks)).astype(jnp.int32)
    replaced = jnp.any(own[None, :] & (jnp.arange(steps)[None, :] <= jnp.arange(steps)[:, None]), axis=1)
    info = jnp.concatenate([x.astype(jnp.int32).reshape(-1) for x in (counts, member, own, replaced)])

    z, lse, w = run_scores(meta, info, queries, cache, fresh)
    lse = exchange_lse(lse)
    pos = positives.astype(jnp.float32).reshape(steps, groups, BLK)

    grad0, tok = run_grads(meta, info, z, queries, lse, 0, 1, lse)
    grad1, tok = run_grads(meta, info, z, queries, lse, 1, blocks - 1, tok)
    chunks = [grad0] + [grad1[i * BLK:(i + 1) * BLK] for i in range(blocks - 1)]
    state = {"term": None}
    pieces = 4
    size = groups // pieces

    def job(i, tok):
        state["term"], tok = run_terms(meta, info, z, w, lse, pos, i * size, size, tok, state["term"])
        return tok

    out = sum_line(chunks, tok, {i: functools.partial(job, i) for i in range(pieces)})
    mine = state["term"].reshape(groups, steps, BLK, width)
    owners = lax.axis_size("cache")
    share = group_rows // owners
    mine = jnp.swapaxes(mine, 0, 1) if share != BLK else mine
    if share == BLK:
        mine = lax.psum_scatter(mine, "cache", scatter_dimension=0, tiled=True)[0]
    else:
        mine = lax.psum_scatter(mine.reshape(steps, group_rows, width), "cache", scatter_dimension=1, tiled=True)
    return mine, jnp.concatenate(out, axis=0)


def solution(mesh):
    return jax.shard_map(
        on_device,
        mesh=mesh,
        in_specs=(
            P(None, "batch", None),
            P(None, "batch"),
            P(None, "batch", None),
            P(None, "batch"),
            P(),
            P("cache", None),
            P("cache", None),
        ),
        out_specs=(P(None, ("batch", "cache"), None), P("cache", None)),
        check_vma=False,
    )
```

```python
import functools
import math

import jax
import jax.numpy as jnp
from jax import lax
from jax.experimental import pallas as pl
from jax.experimental.pallas import tpu as pltpu
from jax.sharding import PartitionSpec as P

BLK = 128
LOW = -1e30
LAGS = (4, 2, 2)
HOME_SLOTS = (8, 14, 18)


def dot(a, b, ca, cb):
    return lax.dot_general(a, b, (((ca,), (cb,)), ((), ())), preferred_element_type=jnp.float32)


def split(x):
    hi = x.astype(jnp.bfloat16)
    return hi, (x - hi.astype(jnp.float32)).astype(jnp.bfloat16)


def as_columns(row):
    return jnp.broadcast_to(row, (BLK, row.shape[1])).T


class Meta:
    def __init__(self, steps, groups, blocks, slab_blocks):
        self.steps, self.groups, self.blocks, self.slab_blocks = steps, groups, blocks, slab_blocks
        self.rows = steps * groups
        self.size = self.rows * blocks

    def count(self, ref, sb, j):
        return ref[sb * self.blocks + j]

    def member(self, ref, sb, j):
        return ref[self.size + sb * self.blocks + j]

    def own(self, ref, s):
        return ref[2 * self.size + s]

    def replaced(self, ref, s):
        return ref[2 * self.size + self.steps + s]

    def me(self, ref):
        return ref[2 * self.size + 2 * self.steps]

    def source(self, ref, s, j):
        return jnp.where((self.replaced(ref, s) > 0) & (j < self.slab_blocks), self.blocks + j, j)


def scores_kernel(meta, group, scale, info, q_hbm, cache_hbm, fresh_hbm, z_ref, w_ref, q_ref, lse_ref,
                  cache_ref, fresh_ref, peak, top, entries, pairs, sem):
    copies = [pltpu.make_async_copy(src, dst, sem.at[i]) for i, (src, dst) in enumerate(
        ((cache_hbm, cache_ref), (fresh_hbm, fresh_ref), (q_hbm, q_ref)))]
    for copy in copies:
        copy.start()

    def collect(sj, carry):
        n_entries, n_pairs = carry
        s, j = sj // meta.blocks, sj % meta.blocks
        m, held = 0, 0
        for b in range(meta.groups):
            sb = s * meta.groups + b
            on = (meta.count(info, sb, j) > 0).astype(jnp.int32)
            pairs[n_pairs] = sb * meta.blocks + j
            n_pairs = n_pairs + on
            held = jnp.where(m % 2 == 0, sb, held)
            entries[n_entries + m // 2] = (held * meta.rows + sb) * meta.blocks + j
            m = m + on

        @pl.when(m % 2 == 1)
        def _():
            entries[n_entries + m // 2] = (held * meta.rows + held) * meta.blocks + j

        return n_entries + (m + 1) // 2, n_pairs

    n_entries, n_pairs = lax.fori_loop(0, meta.steps * meta.blocks, collect, (0, 0))
    for g in range(group):
        entries[n_entries + g] = jnp.where(n_entries > 0, entries[0], 0)
        pairs[n_pairs + g] = 0
    peak[...] = jnp.full(peak.shape, LOW, jnp.float32)

    for copy, src, at in ((copies[0], cache_ref, 0), (copies[1], fresh_ref, meta.blocks)):
        copy.wait()

        def one(k, _, src=src, at=at):
            hi, lo = split(src[pl.ds(pl.multiple_of(k * BLK, BLK), BLK), :])
            w_ref[at + k, :BLK] = hi
            w_ref[at + k, BLK:] = lo
            return 0

        lax.fori_loop(0, src.shape[0] // BLK, one, 0)
    copies[2].wait()

    def score(it, _):
        found = []
        for g in range(group):
            e = entries[it * group + g]
            j, both = e % meta.blocks, e // meta.blocks
            sb0, sb1 = both // meta.rows, both % meta.rows
            left = jnp.concatenate([q_ref[sb0], q_ref[sb1]], axis=0)
            z = dot(left, w_ref[meta.source(info, sb0 // meta.groups, j)], 1, 1)
            found.append((sb0, sb1, j, (z[:, :BLK] + z[:, BLK:]) * scale))
        for sb0, sb1, j, z in found:
            z_ref[sb0, j] = z[:BLK]
            z_ref[sb1, j] = z[BLK:]
            peak[sb0] = jnp.maximum(peak[sb0], z[:BLK])
            peak[sb1] = jnp.maximum(peak[sb1], z[BLK:])
        return 0

    lax.fori_loop(0, (n_entries + group - 1) // group, score, 0)

    def highest(sb, _):
        top[sb] = jnp.broadcast_to(jnp.max(peak[sb], axis=1, keepdims=True), (BLK, BLK))
        peak[sb] = jnp.zeros((BLK, BLK), jnp.float32)
        return 0

    lax.fori_loop(0, meta.rows, highest, 0, unroll=4 if meta.rows % 4 == 0 else 1)

    def add(it, _):
        for g in range(group):
            k = it * group + g
            sb, j = pairs[k] // meta.blocks, pairs[k] % meta.blocks
            c = meta.count(info, sb, j).astype(jnp.float32)
            peak[sb] += jnp.where(k < n_pairs, jnp.exp(z_ref[sb, j] - top[sb]) * c, 0.0)
        return 0

    lax.fori_loop(0, (n_pairs + group - 1) // group, add, 0)

    def finish(sb, _):
        total = jnp.sum(peak[sb], axis=1, keepdims=True)
        lse = jnp.where(total > 0, top[sb][:, :1] + jnp.log(jnp.maximum(total, 1e-30)), LOW)
        lse_ref[pl.ds(sb, 1), :] = jnp.broadcast_to(lse, (BLK, BLK)).T[:1]
        return 0

    lax.fori_loop(0, meta.rows, finish, 0, unroll=4 if meta.rows % 4 == 0 else 1)


def grad_kernel(meta, first, width, info, z_ref, q_ref, lse_ref, dep, out_ref, todo):
    def block(i, _):
        j = first + i
        n = 0
        for sb in range(meta.rows):
            todo[n] = sb
            n = n + meta.member(info, sb, j)
        for g in range(width):
            todo[n + g] = 0
        at = pl.ds(pl.multiple_of(i * BLK, BLK), BLK)
        out_ref[at, :] = jnp.zeros((BLK, out_ref.shape[1]), jnp.float32)

        def step(it, _):
            his, los, rows = [], [], []
            for g in range(width):
                k = it * width + g
                sb = todo[k]
                p = jnp.exp(z_ref[sb, j].T - lse_ref[pl.ds(sb, 1), :])
                hi, lo = split(jnp.where(k < n, p, 0.0))
                his.append(hi)
                los.append(lo)
                rows.append(q_ref[sb])
            left = jnp.concatenate([jnp.concatenate(his, axis=1), jnp.concatenate(los, axis=1)], axis=0)
            acc = dot(left, jnp.concatenate(rows, axis=0), 1, 0)
            out_ref[at, :] += acc[:BLK] + acc[BLK:]
            return 0

        lax.fori_loop(0, (n + width - 1) // width, step, 0)
        return 0

    lax.fori_loop(0, out_ref.shape[0] // BLK, block, 0)


def term_kernel(meta, order, width, info, z_ref, w_ref, lse_ref, pos_ref, dep, *refs):
    outs, (todo, lcol, pcol) = refs[:-3], refs[-3:]
    lane = lax.broadcasted_iota(jnp.int32, (BLK, BLK), 1).astype(jnp.float32)

    def block(i, out_ref, first, stride):
        b = meta.me(info) ^ (first + stride * i) if order else first + stride * i
        n = 0
        for s in range(meta.steps):
            sb = s * meta.groups + b
            lcol[s] = as_columns(lse_ref[pl.ds(sb, 1), :])
            pcol[s] = as_columns(pos_ref[pl.ds(sb, 1), :]) - lane
            out_ref[i, s] = jnp.zeros((BLK, out_ref.shape[3]), jnp.float32)
            for j in range(meta.blocks):
                todo[n] = s * meta.blocks + j
                n = n + (meta.count(info, sb, j) > 0).astype(jnp.int32)
        for g in range(width):
            todo[n + g] = 0

        def step(it, _):
            found = []
            for g in range(width):
                k = it * width + g
                s, j = todo[k] // meta.blocks, todo[k] % meta.blocks
                sb = s * meta.groups + b
                p = jnp.exp(z_ref[sb, j] - lcol[s]) * meta.count(info, sb, j).astype(jnp.float32)
                hot = (meta.own(info, s) > 0) & (j < meta.slab_blocks)
                p = p - jnp.where(pcol[s] == (j * BLK).astype(jnp.float32), hot.astype(jnp.float32), 0.0)
                hi, lo = split(jnp.where(k < n, p, 0.0))
                w = w_ref[meta.source(info, s, j)]
                found.append((s, dot(jnp.concatenate([hi, hi], axis=1), w, 1, 0) + dot(lo, w[:BLK], 1, 0)))
            for s, term in found:
                out_ref[i, s] += term
            return 0

        lax.fori_loop(0, (n + width - 1) // width, step, 0)

    for o, out_ref in enumerate(outs):
        first, stride = (order[o], len(order)) if order else (0, 1)

        def one(i, _, out_ref=out_ref, first=first, stride=stride):
            block(i, out_ref, first, stride)
            return 0

        lax.fori_loop(0, out_ref.shape[0], one, 0)


def params(mib):
    return pltpu.CompilerParams(vmem_limit_bytes=mib * 1024 * 1024)


SMEM = pl.BlockSpec(memory_space=pltpu.SMEM)
VMEM = pl.BlockSpec(memory_space=pltpu.VMEM)
ANY = pl.BlockSpec(memory_space=pl.ANY)


def run_scores(meta, info, queries, cache, fresh):
    width = cache.shape[1]
    group = 4
    n_src = meta.blocks + meta.slab_blocks
    most = meta.steps * meta.blocks * ((meta.groups + 1) // 2)
    return pl.pallas_call(
        functools.partial(scores_kernel, meta, group, 2.0 / math.sqrt(width)),
        in_specs=[SMEM, ANY, ANY, ANY],
        out_specs=[VMEM] * 4,
        out_shape=[
            pltpu.VMEM((meta.rows, meta.blocks, BLK, BLK), jnp.float32),
            pltpu.VMEM((n_src, 2 * BLK, width), jnp.bfloat16),
            pltpu.VMEM((meta.rows, BLK, width), jnp.bfloat16),
            pltpu.VMEM((meta.rows, BLK), jnp.float32),
        ],
        scratch_shapes=[
            pltpu.VMEM(cache.shape, jnp.float32),
            pltpu.VMEM(fresh.shape, jnp.float32),
            pltpu.VMEM((meta.rows, BLK, BLK), jnp.float32),
            pltpu.VMEM((meta.rows, BLK, BLK), jnp.float32),
            pltpu.SMEM((most + group + 1,), jnp.int32),
            pltpu.SMEM((meta.size + group,), jnp.int32),
            pltpu.SemaphoreType.DMA((3,)),
        ],
        compiler_params=params(20),
        name="scores",
    )(info, queries.reshape(meta.rows, BLK, width), cache, fresh)


def run_grads(meta, info, z, q, lse, first, count, dep):
    group = 4
    return pl.pallas_call(
        functools.partial(grad_kernel, meta, first, group),
        in_specs=[SMEM, VMEM, VMEM, VMEM, ANY],
        out_specs=VMEM,
        out_shape=pltpu.VMEM((count * BLK, q.shape[2]), jnp.float32),
        scratch_shapes=[pltpu.SMEM((meta.rows + group,), jnp.int32)],
        compiler_params=params(10),
        name="cache_grad",
    )(info, z, q, lse, dep)


def run_terms(meta, info, z, w, lse, pos, order, dep):
    group = 4
    n_out = max(1, len(order))
    shape = (meta.groups // n_out, meta.steps, BLK, w.shape[2])
    return pl.pallas_call(
        functools.partial(term_kernel, meta, order, group),
        in_specs=[SMEM, VMEM, VMEM, VMEM, VMEM, ANY],
        out_specs=[VMEM] * n_out,
        out_shape=[pltpu.VMEM(shape, jnp.float32)] * n_out,
        scratch_shapes=[
            pltpu.SMEM((meta.steps * meta.blocks + group,), jnp.int32),
            pltpu.VMEM((meta.steps, BLK, BLK), jnp.float32),
            pltpu.VMEM((meta.steps, BLK, BLK), jnp.float32),
        ],
        compiler_params=params(10),
        name="query_term",
    )(info, z, w, lse, pos, dep)


def exchange_lse(lse):
    n = lax.axis_size("cache")
    bit = 1
    while bit < n:
        lse = jnp.logaddexp(lse, lax.ppermute(lse, "cache", [(i, i ^ bit) for i in range(n)]))
        bit *= 2
    return lse


def barrier(*values):
    return lax.optimization_barrier(tuple(values))


def token(x):
    return lax.slice(x, (0,) * x.ndim, (1,) * x.ndim).reshape(1, 1)


def sum_line(chunks, n, jobs):
    if lax.axis_size("batch") != 4:
        tok = token(chunks[0])
        for t in sorted(jobs):
            tok = jobs[t](tok)
        return [lax.psum(c, "batch") for c in chunks]
    at = lax.axis_index("batch")
    end = (at == 0) | (at == 3)
    lag_in, lag_mid, lag_out = LAGS
    late = lag_in + lag_mid
    swap, mid, inner, total, out = {}, {}, {}, {}, {}
    prev = [token(chunks[0])]
    for t in range(n + late + lag_out):
        u, k, o = t - lag_in, t - late, t - late - lag_out
        ops = []
        if 0 <= u < n:
            ops += [chunks[u], swap[u]]
        if 0 <= o < n:
            ops += [total[o], swap[o + late]]
        if 0 <= k < n:
            ops += [inner[k], mid[k]]
        if t < n:
            ops += [chunks[t]]
        ops = list(barrier(*ops, *prev)[:len(ops)])
        away = None
        if 0 <= u < n:
            inner[u] = ops.pop(0) + ops.pop(0)
        if 0 <= o < n:
            own = ops.pop(0)
            out[o] = jnp.where(end, ops.pop(0), own)
        if 0 <= k < n:
            away = total[k] = ops.pop(0) + ops.pop(0)
        if t < n:
            chunk = ops.pop(0)
            away = chunk if away is None else jnp.where(end, chunk, away)
        new = [] if away is None else [away]
        if 0 <= u < n:
            new.append(inner[u])
        if 0 <= o < n:
            new.append(out[o])
        if not new:
            continue
        new = list(barrier(*new))
        prev = [token(v) for v in new]
        if away is not None:
            swap[t] = lax.ppermute(new.pop(0), "batch", [(0, 1), (1, 0), (2, 3), (3, 2)])
        if 0 <= u < n:
            inner[u] = new.pop(0)
            mid[u] = lax.ppermute(inner[u], "batch", [(1, 2), (2, 1)])
        if 0 <= o < n:
            out[o] = new.pop(0)
        if t in jobs:
            prev.append(jobs[t](prev[0]))
    return [out[k] for k in range(n)]


class HomeSum:
    def __init__(self, odd, even):
        self.n = lax.axis_size("cache")
        self.even = even
        self.got = self.move(odd, 1)
        self.bits = [1 << i for i in range(1, self.n.bit_length() - 1)]
        self.cur = None

    def move(self, x, bit):
        return lax.ppermute(x, "cache", [(i, i ^ bit) for i in range(self.n)])

    def send(self, tok):
        orders = (self.bits, self.bits[::-1])
        if self.cur is None:
            even, got = barrier(self.even, self.got, tok)[:2]
            half = even.shape[2] // 2
            self.cur = []
            for lo in (0, half):
                both = even[:, :, lo:lo + half] + got[:, :, lo:lo + half]
                self.cur.append({2 * i: both[i] for i in range(self.n // 2)})
            self.stage = 0
        else:
            self.receive(tok)
        self.away = []
        if self.stage == len(self.bits):
            return token(self.cur[0][0])
        self.moved = []
        toks = []
        for cur, order in zip(self.cur, orders):
            bit = order[self.stage]
            far = [r for r in sorted(cur) if r & bit]
            stack = barrier(jnp.stack([cur[r] for r in far]))[0]
            toks.append(token(stack))
            self.moved.append((bit, far, self.move(stack, bit)))
        self.stage += 1
        return toks[0] + toks[1]

    def receive(self, tok):
        arrived = barrier(*[m[2] for m in self.moved], tok)
        for i, (bit, far, _) in enumerate(self.moved):
            cur = self.cur[i]
            self.cur[i] = {r ^ bit: cur[r ^ bit] + arrived[i][f] for f, r in enumerate(far)}

    def result(self):
        return jnp.concatenate([cur[0] for cur in self.cur], axis=1)


def on_device(queries, positives, block_list, block_count, refresh_owner, cache, fresh):
    steps, group_rows, width = queries.shape
    groups = group_rows // BLK
    blocks, slab_blocks = cache.shape[0] // BLK, fresh.shape[0] // BLK
    meta = Meta(steps, groups, blocks, slab_blocks)
    me = lax.axis_index("cache")
    block_ids = me * blocks + jnp.arange(blocks, dtype=jnp.int32)
    valid = jnp.arange(block_list.shape[2], dtype=jnp.int32)[None, None, :] < block_count[:, :, None]
    member = jnp.any((block_list[..., None] == block_ids) & valid[..., None], axis=2)
    own = refresh_owner == me
    counts = member.astype(jnp.int32) + (own[:, None, None] & (jnp.arange(blocks) < slab_blocks)).astype(jnp.int32)
    replaced = jnp.any(own[None, :] & (jnp.arange(steps)[None, :] <= jnp.arange(steps)[:, None]), axis=1)
    info = jnp.concatenate([x.astype(jnp.int32).reshape(-1) for x in (counts, member, own, replaced, me)])

    z, w, q, own_lse = run_scores(meta, info, queries, cache, fresh)
    lse = exchange_lse(own_lse)
    pos = positives.astype(jnp.float32).reshape(meta.rows, BLK)

    half = BLK // 2
    early = min(2, blocks)
    chunks = []

    def fill(first, count, tok):
        grad = run_grads(meta, info, z, q, lse, first, count, tok)
        chunks.extend(grad[i:i + half] for i in range(0, count * BLK, half))
        return token(grad)

    fill(0, early, lse)
    owners = lax.axis_size("cache")
    share = group_rows // owners
    jobs = {}
    state = []
    fast = share == BLK and owners == groups and owners & (owners - 1) == 0 and owners > 2

    def rest(tok):
        if early < blocks:
            tok = fill(early, blocks - early, tok)
        if fast:
            odd, even = run_terms(meta, info, z, w, lse, pos, (1, 0), tok)
            state.append(HomeSum(odd, even))
            tok = token(even)
        return tok

    jobs[min(LAGS[0], len(chunks)) - 1] = rest
    if fast:
        for t in HOME_SLOTS:
            jobs[t] = lambda tok: state[0].send(tok)
    out = sum_line(chunks, 2 * blocks, jobs)
    if fast:
        mine = state[0].result()
    else:
        term = run_terms(meta, info, z, w, lse, pos, (), lse)[0]
        term = jnp.swapaxes(term, 0, 1).reshape(steps, group_rows, width)
        mine = lax.psum_scatter(term, "cache", scatter_dimension=1, tiled=True)
    return mine, jnp.concatenate(out, axis=0)


def solution(mesh):
    return jax.shard_map(
        on_device,
        mesh=mesh,
        in_specs=(
            P(None, "batch", None),
            P(None, "batch"),
            P(None, "batch", None),
            P(None, "batch"),
            P(),
            P("cache", None),
            P("cache", None),
        ),
        out_specs=(P(None, ("batch", "cache"), None), P("cache", None)),
        check_vma=False,
    )
```

```python
import functools
import math

import jax
import jax.numpy as jnp
from jax import lax
from jax.experimental import pallas as pl
from jax.experimental.pallas import tpu as pltpu
from jax.sharding import PartitionSpec as P

BLK = 128
LOW = -1e30
LAGS = (4, 2, 2)
HOME_SLOTS = (8, 15, 20)
SLOT_FLOPS = 4_000_000_000


def dot(a, b, ca, cb):
    return lax.dot_general(a, b, (((ca,), (cb,)), ((), ())), preferred_element_type=jnp.float32)


def split(x):
    hi = x.astype(jnp.bfloat16)
    return hi, (x - hi.astype(jnp.float32)).astype(jnp.bfloat16)


def as_columns(row):
    return jnp.broadcast_to(row, (BLK, row.shape[1])).T


class Meta:
    def __init__(self, steps, groups, blocks, slab_blocks):
        self.steps, self.groups, self.blocks, self.slab_blocks = steps, groups, blocks, slab_blocks
        self.rows = steps * groups
        self.size = self.rows * blocks

    def flags(self, owner, out):
        me = lax.axis_index("cache")
        seen = 0
        for s in range(self.steps):
            own = (owner[s] == me).astype(jnp.int32)
            seen = jnp.maximum(seen, own)
            out[s] = own
            out[self.steps + s] = seen

    def count(self, member, flags, s, sb, j):
        return member[sb, j] + jnp.where(j < self.slab_blocks, flags[s], 0)

    def source(self, flags, s, j):
        return jnp.where((flags[self.steps + s] > 0) & (j < self.slab_blocks), self.blocks + j, j)


def scores_kernel(meta, group, scale, member, owner, q_hbm, cache_hbm, fresh_hbm, z_ref, w_ref, q_ref, lse_ref,
                  cache_ref, fresh_ref, peak, top, flags, entries, pairs, sem):
    copies = [pltpu.make_async_copy(src, dst, sem.at[i]) for i, (src, dst) in enumerate(
        ((cache_hbm, cache_ref), (fresh_hbm, fresh_ref), (q_hbm, q_ref)))]
    for copy in copies:
        copy.start()
    meta.flags(owner, flags)

    def collect(sj, carry):
        n_entries, n_pairs = carry
        s, j = sj // meta.blocks, sj % meta.blocks
        m, held = 0, 0
        for b in range(meta.groups):
            sb = s * meta.groups + b
            on = (meta.count(member, flags, s, sb, j) > 0).astype(jnp.int32)
            pairs[n_pairs] = sb * meta.blocks + j
            n_pairs = n_pairs + on
            held = jnp.where(m % 2 == 0, sb, held)
            entries[n_entries + m // 2] = (held * meta.rows + sb) * meta.blocks + j
            m = m + on

        @pl.when(m % 2 == 1)
        def _():
            entries[n_entries + m // 2] = (held * meta.rows + held) * meta.blocks + j

        return n_entries + (m + 1) // 2, n_pairs

    n_entries, n_pairs = lax.fori_loop(0, meta.steps * meta.blocks, collect, (0, 0))
    for g in range(group):
        entries[n_entries + g] = jnp.where(n_entries > 0, entries[0], 0)
        pairs[n_pairs + g] = 0
    peak[...] = jnp.full(peak.shape, LOW, jnp.float32)

    for copy, src, at in ((copies[0], cache_ref, 0), (copies[1], fresh_ref, meta.blocks)):
        copy.wait()

        def one(k, _, src=src, at=at):
            hi, lo = split(src[pl.ds(pl.multiple_of(k * BLK, BLK), BLK), :])
            w_ref[at + k, :BLK] = hi
            w_ref[at + k, BLK:] = lo
            return 0

        lax.fori_loop(0, src.shape[0] // BLK, one, 0)
    copies[2].wait()

    def score(it, _):
        found = []
        for g in range(group):
            e = entries[it * group + g]
            j, both = e % meta.blocks, e // meta.blocks
            sb0, sb1 = both // meta.rows, both % meta.rows
            left = jnp.concatenate([q_ref[sb0], q_ref[sb1]], axis=0)
            z = dot(left, w_ref[meta.source(flags, sb0 // meta.groups, j)], 1, 1)
            found.append((sb0, sb1, j, (z[:, :BLK] + z[:, BLK:]) * scale))
        for sb0, sb1, j, z in found:
            z_ref[sb0, j] = z[:BLK]
            z_ref[sb1, j] = z[BLK:]
            peak[sb0] = jnp.maximum(peak[sb0], z[:BLK])
            peak[sb1] = jnp.maximum(peak[sb1], z[BLK:])
        return 0

    lax.fori_loop(0, (n_entries + group - 1) // group, score, 0)

    def highest(sb, _):
        top[sb] = jnp.broadcast_to(jnp.max(peak[sb], axis=1, keepdims=True), (BLK, BLK))
        peak[sb] = jnp.zeros((BLK, BLK), jnp.float32)
        return 0

    lax.fori_loop(0, meta.rows, highest, 0, unroll=4 if meta.rows % 4 == 0 else 1)

    def add(it, _):
        for g in range(group):
            k = it * group + g
            sb, j = pairs[k] // meta.blocks, pairs[k] % meta.blocks
            c = meta.count(member, flags, sb // meta.groups, sb, j).astype(jnp.float32)
            peak[sb] += jnp.where(k < n_pairs, jnp.exp(z_ref[sb, j] - top[sb]) * c, 0.0)
        return 0

    lax.fori_loop(0, (n_pairs + group - 1) // group, add, 0)

    def finish(sb, _):
        total = jnp.sum(peak[sb], axis=1, keepdims=True)
        lse = jnp.where(total > 0, top[sb][:, :1] + jnp.log(jnp.maximum(total, 1e-30)), LOW)
        lse_ref[pl.ds(sb, 1), :] = jnp.broadcast_to(lse, (BLK, BLK)).T[:1]
        return 0

    lax.fori_loop(0, meta.rows, finish, 0, unroll=4 if meta.rows % 4 == 0 else 1)


def grad_kernel(meta, first, width, member, z_ref, q_ref, lse_ref, dep, out_ref, todo):
    def block(i, _):
        j = first + i
        n = 0
        for sb in range(meta.rows):
            todo[n] = sb
            n = n + member[sb, j]
        for g in range(width):
            todo[n + g] = 0
        at = pl.ds(pl.multiple_of(i * BLK, BLK), BLK)
        out_ref[at, :] = jnp.zeros((BLK, out_ref.shape[1]), jnp.float32)

        def step(it, _):
            his, los, rows = [], [], []
            for g in range(width):
                k = it * width + g
                sb = todo[k]
                p = jnp.exp(z_ref[sb, j].T - lse_ref[pl.ds(sb, 1), :])
                hi, lo = split(jnp.where(k < n, p, 0.0))
                his.append(hi)
                los.append(lo)
                rows.append(q_ref[sb])
            left = jnp.concatenate([jnp.concatenate(his, axis=1), jnp.concatenate(los, axis=1)], axis=0)
            acc = dot(left, jnp.concatenate(rows, axis=0), 1, 0)
            out_ref[at, :] += acc[:BLK] + acc[BLK:]
            return 0

        lax.fori_loop(0, (n + width - 1) // width, step, 0)
        return 0

    lax.fori_loop(0, out_ref.shape[0] // BLK, block, 0)


def term_kernel(meta, order, width, member, owner, z_ref, w_ref, lse_ref, pos_ref, dep, *refs):
    outs, (flags, todo, lcol, pcol) = refs[:-4], refs[-4:]
    meta.flags(owner, flags)
    lane = lax.broadcasted_iota(jnp.int32, (BLK, BLK), 1).astype(jnp.float32)

    def block(i, out_ref, first, stride):
        b = lax.axis_index("cache") ^ (first + stride * i) if order else first + stride * i
        n = 0
        for s in range(meta.steps):
            sb = s * meta.groups + b
            lcol[s] = as_columns(lse_ref[pl.ds(sb, 1), :])
            pcol[s] = as_columns(pos_ref[s:s + 1, pl.ds(pl.multiple_of(b * BLK, BLK), BLK)].astype(jnp.float32)) - lane
            out_ref[i, s] = jnp.zeros((BLK, out_ref.shape[3]), jnp.float32)
            for j in range(meta.blocks):
                todo[n] = s * meta.blocks + j
                n = n + (meta.count(member, flags, s, sb, j) > 0).astype(jnp.int32)
        for g in range(width):
            todo[n + g] = 0

        def step(it, _):
            found = []
            for g in range(width):
                k = it * width + g
                s, j = todo[k] // meta.blocks, todo[k] % meta.blocks
                sb = s * meta.groups + b
                p = jnp.exp(z_ref[sb, j] - lcol[s]) * meta.count(member, flags, s, sb, j).astype(jnp.float32)
                hot = (flags[s] > 0) & (j < meta.slab_blocks)
                p = p - jnp.where(pcol[s] == (j * BLK).astype(jnp.float32), hot.astype(jnp.float32), 0.0)
                hi, lo = split(jnp.where(k < n, p, 0.0))
                w = w_ref[meta.source(flags, s, j)]
                found.append((s, dot(jnp.concatenate([hi, hi], axis=1), w, 1, 0) + dot(lo, w[:BLK], 1, 0)))
            for s, term in found:
                out_ref[i, s] += term
            return 0

        lax.fori_loop(0, (n + width - 1) // width, step, 0)

    for o, out_ref in enumerate(outs):
        first, stride = (order[o], len(order)) if order else (0, 1)

        def one(i, _, out_ref=out_ref, first=first, stride=stride):
            block(i, out_ref, first, stride)
            return 0

        lax.fori_loop(0, out_ref.shape[0], one, 0)


def params(mib):
    return pltpu.CompilerParams(vmem_limit_bytes=mib * 1024 * 1024)


def free():
    return pl.CostEstimate(flops=0, bytes_accessed=0, transcendentals=0)


SMEM = pl.BlockSpec(memory_space=pltpu.SMEM)
VMEM = pl.BlockSpec(memory_space=pltpu.VMEM)
ANY = pl.BlockSpec(memory_space=pl.ANY)
HBM = pl.BlockSpec(memory_space=pltpu.HBM)


def run_scores(meta, member, owner, queries, cache, fresh):
    width = cache.shape[1]
    group = 4
    n_src = meta.blocks + meta.slab_blocks
    most = meta.steps * meta.blocks * ((meta.groups + 1) // 2)
    return pl.pallas_call(
        functools.partial(scores_kernel, meta, group, 2.0 / math.sqrt(width)),
        in_specs=[SMEM, SMEM, HBM, HBM, HBM],
        out_specs=[VMEM] * 4,
        out_shape=[
            pltpu.VMEM((meta.rows, meta.blocks, BLK, BLK), jnp.float32),
            pltpu.VMEM((n_src, 2 * BLK, width), jnp.bfloat16),
            pltpu.VMEM((meta.rows, BLK, width), jnp.bfloat16),
            pltpu.VMEM((meta.rows, BLK), jnp.float32),
        ],
        scratch_shapes=[
            pltpu.VMEM(cache.shape, jnp.float32),
            pltpu.VMEM(fresh.shape, jnp.float32),
            pltpu.VMEM((meta.rows, BLK, BLK), jnp.float32),
            pltpu.VMEM((meta.rows, BLK, BLK), jnp.float32),
            pltpu.SMEM((2 * meta.steps,), jnp.int32),
            pltpu.SMEM((most + group + 1,), jnp.int32),
            pltpu.SMEM((meta.size + group,), jnp.int32),
            pltpu.SemaphoreType.DMA((3,)),
        ],
        compiler_params=params(20),
        name="scores",
    )(member, owner, *(pltpu.with_memory_space_constraint(x, pltpu.HBM)
                       for x in (queries.reshape(meta.rows, BLK, width), cache, fresh)))


def run_grads(meta, member, z, q, lse, first, count, dep):
    group = 4
    return pl.pallas_call(
        functools.partial(grad_kernel, meta, first, group),
        in_specs=[SMEM, VMEM, VMEM, VMEM, ANY],
        out_specs=VMEM,
        out_shape=pltpu.VMEM((count * BLK, q.shape[2]), jnp.float32),
        scratch_shapes=[pltpu.SMEM((meta.rows + group,), jnp.int32)],
        compiler_params=params(10),
        cost_estimate=free(),
        name="cache_grad",
    )(member, z, q, lse, dep)


def run_terms(meta, member, owner, z, w, lse, pos, order, dep):
    group = 4
    n_out = max(1, len(order))
    shape = (meta.groups // n_out, meta.steps, BLK, w.shape[2])
    return pl.pallas_call(
        functools.partial(term_kernel, meta, order, group),
        in_specs=[SMEM, SMEM, VMEM, VMEM, VMEM, VMEM, ANY],
        out_specs=[VMEM] * n_out,
        out_shape=[pltpu.VMEM(shape, jnp.float32)] * n_out,
        scratch_shapes=[
            pltpu.SMEM((2 * meta.steps,), jnp.int32),
            pltpu.SMEM((meta.steps * meta.blocks + group,), jnp.int32),
            pltpu.VMEM((meta.steps, BLK, BLK), jnp.float32),
            pltpu.VMEM((meta.steps, BLK, BLK), jnp.float32),
        ],
        compiler_params=params(10),
        cost_estimate=free(),
        name="query_term",
    )(member, owner, z, w, lse, pos, dep)


def small(kernel, inputs, n_deps, outs, name, aliases=None, flops=0):
    n_vmem = len(inputs) - n_deps
    return pl.pallas_call(
        kernel,
        in_specs=[VMEM] * n_vmem + [ANY] * n_deps,
        out_specs=[VMEM] * len(outs),
        out_shape=[pltpu.VMEM(shape, jnp.float32) for shape in outs],
        input_output_aliases=aliases or {},
        compiler_params=params(4),
        cost_estimate=pl.CostEstimate(flops=flops, bytes_accessed=0, transcendentals=0),
        name=name,
    )(*inputs)


def merge_kernel(*refs):
    xs, out_ref = [r[...] for r in refs[:-1]], refs[-1]
    top = functools.reduce(jnp.maximum, xs)
    out_ref[...] = top + jnp.log(sum(jnp.exp(x - top) for x in xs))


def exchange_lse(lse):
    n = lax.axis_size("cache")
    bits = [1 << i for i in range(n.bit_length() - 1)]
    rounds = [bits[:1]] + [bits[i:i + 2] for i in range(1, len(bits), 2)]
    for some in rounds:
        partners = some if len(some) == 1 else [some[0], some[1], some[0] | some[1]]
        got = [lax.ppermute(lse, "cache", [(i, i ^ p) for i in range(n)]) for p in partners]
        lse = small(merge_kernel, [lse] + got, 0, [lse.shape], "merge_lse")[0]
    return lse


class Line:
    def __init__(self, n, rows, width):
        self.n, self.rows, self.width = n, rows, width
        self.lag_in, self.lag_mid, self.lag_out = LAGS
        self.late = self.lag_in + self.lag_mid
        self.slots = n + self.late + self.lag_out
        self.swap, self.mid, self.inner, self.total = {}, {}, {}, {}
        self.out = None

    def begin(self, array):
        self.swap[0] = lax.ppermute(array, "batch", [(0, 1), (1, 0), (2, 3), (3, 2)])

    def slot(self, t, chunk, deps):
        n, rows = self.n, self.rows
        u, k, o = t - self.lag_in, t - self.late, t - self.late - self.lag_out
        inputs, plan, outs = [], [], []

        def take(x):
            inputs.append(x)
            return len(inputs) - 1

        def give(shape=(rows, self.width)):
            outs.append(shape)
            return len(outs) - 1

        aliases = {}
        if 0 <= u < n:
            array, first = chunk(u)
            came, row = (self.swap[0], u * rows) if u < self.lag_in else (self.swap[u], 0)
            plan.append(("in", take(array), first, take(came), row, give()))
        if 0 <= k < n:
            plan.append(("sum", take(self.inner[k]), take(self.mid[k]), give()))
        if t < n:
            array, first = chunk(t)
            plan.append(("away", take(array), first, give()))
        if 0 <= o < n:
            args = take(self.total[o]), take(self.swap[o + self.late])
            old = None if self.out is None else take(self.out)
            new = give((n * rows, self.width))
            if old is not None:
                aliases = {old: new}
            plan.append(("out",) + args + (new,))
        n_in = len(inputs)

        def kernel(*refs):
            at = lax.axis_index("batch")
            end = (at == 0) | (at == 3)
            res = refs[n_in + len(deps):]
            total = None
            for what, *a in plan:
                if what == "in":
                    res[a[4]][...] = refs[a[0]][a[1]:a[1] + rows, :] + refs[a[2]][a[3]:a[3] + rows, :]
                elif what == "sum":
                    total = refs[a[0]][...] + refs[a[1]][...]
                    res[a[2]][...] = total
                elif what == "away":
                    value = refs[a[0]][a[1]:a[1] + rows, :]
                    res[a[2]][...] = value if total is None else jnp.where(end, value, total)
                else:
                    res[a[2]][o * rows:(o + 1) * rows, :] = jnp.where(end, refs[a[1]][...], refs[a[0]][...])

        got = small(kernel, inputs + list(deps), len(deps), outs, "line_slot", aliases, SLOT_FLOPS)
        away = None
        for what, *a in plan:
            if what == "in":
                self.inner[u] = got[a[4]]
            elif what == "sum":
                away = self.total[k] = got[a[2]]
            elif what == "away":
                away = got[a[2]]
            else:
                self.out = got[a[2]]
        if away is not None:
            self.swap[t] = lax.ppermute(away, "batch", [(0, 1), (1, 0), (2, 3), (3, 2)])
        if 0 <= u < n:
            self.mid[u] = lax.ppermute(self.inner[u], "batch", [(1, 2), (2, 1)])
        return got[0]


class HomeSum:
    def __init__(self, odd, even):
        self.n = lax.axis_size("cache")
        self.odd, self.even = odd, even
        self.steps, self.rows, self.width = even.shape[1:]
        self.bits = [1 << i for i in range(1, self.n.bit_length() - 1)]
        self.stage = 0

    def move(self, x, bit):
        return lax.ppermute(x, "cache", [(i, i ^ bit) for i in range(self.n)])

    def start(self, dep):
        def kernel(*refs):
            pass

        odd = small(kernel, [self.odd, dep], 1, [self.odd.shape], "home_start", {0: 0})[0]
        self.got = self.move(odd, 1)

    def step(self, dep):
        half = self.rows // 2
        orders = (self.bits, self.bits[::-1])
        last = self.stage == len(self.bits)
        if self.stage == 0:
            inputs = [self.even, self.got]
            sources = [({2 * i: i for i in range(self.n // 2)}, 0, 1, h * half) for h in (0, 1)]
        else:
            inputs, sources = [], []
            for (place, keep), got in zip(self.kept, self.moved):
                sources.append((place, len(inputs), len(inputs) + 1, 0))
                inputs += [keep, got]
        writes, outs, kept = [], [], []
        for h, (place, a, b, first) in enumerate(sources):
            if last:
                writes.append((h, 0, 0, h * half))
                continue
            bit = orders[h][self.stage]
            far = [r for r in sorted(place) if r & bit]
            near = [r for r in sorted(place) if not r & bit]
            for rs in (far, near):
                outs.append((len(rs), self.steps, half, self.width))
                writes += [(h, r, (len(outs) - 1, i), None) for i, r in enumerate(rs)]
            kept.append({r: i for i, r in enumerate(near)})
        if last:
            outs = [(self.steps, self.rows, self.width)]
        n_in, steps = len(inputs), self.steps

        def kernel(*refs):
            res = refs[n_in + 1:]
            for h, r, to, at in writes:
                place, a, b, first = sources[h]
                i = place[r]

                def one(s, _, a=a, b=b, i=i, first=first, to=to, at=at):
                    value = refs[a][i, s, first:first + half, :] + refs[b][i, s, first:first + half, :]
                    if at is None:
                        res[to[0]][to[1], s] = value
                    else:
                        res[0][s, at:at + half, :] = value
                    return 0

                lax.fori_loop(0, steps, one, 0)

        got = small(kernel, inputs + [dep], 1, outs, "home_sum")
        if last:
            return got[0]
        self.kept = [(kept[h], got[2 * h + 1]) for h in (0, 1)]
        self.moved = [self.move(got[2 * h], orders[h][self.stage]) for h in (0, 1)]
        self.stage += 1
        return got[1]


def on_device(queries, positives, block_list, block_count, refresh_owner, cache, fresh):
    steps, group_rows, width = queries.shape
    groups = group_rows // BLK
    blocks, slab_blocks = cache.shape[0] // BLK, fresh.shape[0] // BLK
    meta = Meta(steps, groups, blocks, slab_blocks)
    me = lax.axis_index("cache")
    block_ids = me * blocks + jnp.arange(blocks, dtype=jnp.int32)
    valid = jnp.arange(block_list.shape[2], dtype=jnp.int32)[None, None, :] < block_count[:, :, None]
    member = jnp.any((block_list[..., None] == block_ids) & valid[..., None], axis=2)
    member = member.astype(jnp.int32).reshape(meta.rows, blocks)
    owner = refresh_owner.astype(jnp.int32)

    z, w, q, own_lse = run_scores(meta, member, owner, queries, cache, fresh)
    lse = exchange_lse(own_lse)

    half = BLK // 2
    early = min(LAGS[0] * half // BLK, blocks)
    grads = [run_grads(meta, member, z, q, lse, 0, early, lse)]
    owners = lax.axis_size("cache")
    share = group_rows // owners
    fast = share == BLK and owners == groups and owners & (owners - 1) == 0 and owners > 2
    home = mine = None

    def chunk(k):
        n = early * BLK // half
        return (grads[0], k * half) if k < n else (grads[1], (k - n) * half)

    def rest(dep):
        grads.append(run_grads(meta, member, z, q, lse, early, blocks - early, dep))
        if not fast:
            return grads[1], None
        odd, even = run_terms(meta, member, owner, z, w, lse, positives, (1, 0), grads[1])
        return even, HomeSum(odd, even)

    if lax.axis_size("batch") == 4 and blocks > early:
        line = Line(2 * blocks, half, width)
        line.begin(grads[0])
        dep, home = rest(grads[0])
        deps = [dep]
        for t in range(LAGS[0], line.slots):
            deps = [line.slot(t, chunk, deps)]
            if t == LAGS[0] and fast:
                home.start(deps[0])
            if fast and t in HOME_SLOTS:
                deps.append(home.step(deps[0]))
                mine = deps[-1]
        grad = line.out
    else:
        _, home = rest(lse)
        if fast:
            home.start(lse)
        grad = lax.psum(jnp.concatenate(grads, axis=0), "batch")
    if fast:
        while home.stage < len(home.bits):
            home.step(lse)
        if mine is None or mine.ndim != 3:
            mine = home.step(lse)
    else:
        term = run_terms(meta, member, owner, z, w, lse, positives, (), lse)[0]
        term = jnp.swapaxes(term, 0, 1).reshape(steps, group_rows, width)
        mine = lax.psum_scatter(term, "cache", scatter_dimension=1, tiled=True)
    return mine, grad


def solution(mesh):
    return jax.shard_map(
        on_device,
        mesh=mesh,
        in_specs=(
            P(None, "batch", None),
            P(None, "batch"),
            P(None, "batch", None),
            P(None, "batch"),
            P(),
            P("cache", None),
            P("cache", None),
        ),
        out_specs=(P(None, ("batch", "cache"), None), P("cache", None)),
        check_vma=False,
    )
```

```python
import functools
import math

import jax
import jax.numpy as jnp
from jax import lax
from jax.experimental import pallas as pl
from jax.experimental.pallas import tpu as pltpu
from jax.sharding import PartitionSpec as P

BLK = 128
LOW = -1e30
LAGS = (4, 3, 2)
HOME_SLOTS = (7, 14, 18)
START_SLOT = 4
TERM_SLOTS = ()
PARTS = 1 + len(TERM_SLOTS)
SLOT_FLOPS = 4_000_000_000


def dot(a, b, ca, cb):
    return lax.dot_general(a, b, (((ca,), (cb,)), ((), ())), preferred_element_type=jnp.float32)


def split(x):
    hi = x.astype(jnp.bfloat16)
    return hi, (x - hi.astype(jnp.float32)).astype(jnp.bfloat16)


class Meta:
    def __init__(self, steps, groups, blocks, slab_blocks):
        self.steps, self.groups, self.blocks, self.slab_blocks = steps, groups, blocks, slab_blocks
        self.rows = steps * groups
        self.size = self.rows * blocks

    def flags(self, owner, out):
        me = lax.axis_index("cache")
        seen = 0
        for s in range(self.steps):
            own = (owner[s] == me).astype(jnp.int32)
            seen = jnp.maximum(seen, own)
            out[s] = own
            out[self.steps + s] = seen

    def count(self, member, flags, s, sb, j):
        return member[sb, j] + jnp.where(j < self.slab_blocks, flags[s], 0)

    def source(self, flags, s, j):
        return jnp.where((flags[self.steps + s] > 0) & (j < self.slab_blocks), self.blocks + j, j)


def scores_kernel(meta, group, scale, member, owner, q_hbm, cache_hbm, fresh_hbm, z_ref, w_ref, q_ref, lse_ref, entries,
                  cache_ref, fresh_ref, peak, total, flags, pairs, sem):
    copies = [pltpu.make_async_copy(src, dst, sem.at[i]) for i, (src, dst) in enumerate(
        ((cache_hbm, cache_ref), (fresh_hbm, fresh_ref), (q_hbm, q_ref)))]
    for copy in copies:
        copy.start()
    meta.flags(owner, flags)

    def collect(sj, carry):
        n_entries, n_pairs = carry
        s, j = sj // meta.blocks, sj % meta.blocks
        m, held = 0, 0
        for b in range(meta.groups):
            sb = s * meta.groups + b
            on = (meta.count(member, flags, s, sb, j) > 0).astype(jnp.int32)
            pairs[n_pairs] = sb * meta.blocks + j
            n_pairs = n_pairs + on
            held = jnp.where(m % 2 == 0, sb, held)
            entries[n_entries + m // 2] = (held * meta.rows + sb) * meta.blocks + j
            m = m + on

        @pl.when(m % 2 == 1)
        def _():
            entries[n_entries + m // 2] = (held * meta.rows + held) * meta.blocks + j

        return n_entries + (m + 1) // 2, n_pairs

    n_entries, n_pairs = lax.fori_loop(0, meta.steps * meta.blocks, collect, (0, 0))
    for g in range(group):
        entries[n_entries + g] = jnp.where(n_entries > 0, entries[0], 0)
        pairs[n_pairs + g] = 0
    entries[entries.shape[0] - 1] = n_entries
    peak[...] = jnp.full(peak.shape, LOW, jnp.float32)
    total[...] = jnp.zeros(total.shape, jnp.float32)

    for copy, src, at in ((copies[0], cache_ref, 0), (copies[1], fresh_ref, meta.blocks)):
        copy.wait()

        def one(k, _, src=src, at=at):
            hi, lo = split(src[pl.ds(pl.multiple_of(k * BLK, BLK), BLK), :])
            w_ref[at + k, :BLK] = hi
            w_ref[at + k, BLK:] = lo
            return 0

        lax.fori_loop(0, src.shape[0] // BLK, one, 0)
    copies[2].wait()

    def score(it, _):
        found = []
        for g in range(group):
            e = entries[it * group + g]
            j, both = e % meta.blocks, e // meta.blocks
            sb0, sb1 = both // meta.rows, both % meta.rows
            right = jnp.concatenate([q_ref[sb0], q_ref[sb1]], axis=0)
            z = dot(w_ref[meta.source(flags, sb0 // meta.groups, j)], right, 1, 1)
            found.append((sb0, sb1, j, (z[:BLK] + z[BLK:]) * scale))
        for sb0, sb1, j, z in found:
            for sb, one in ((sb0, z[:, :BLK]), (sb1, z[:, BLK:])):
                z_ref[sb, j] = one
                row = pl.ds(sb, 1)
                peak[row, :] = jnp.maximum(peak[row, :], jnp.max(one, axis=0, keepdims=True))
        return 0

    lax.fori_loop(0, (n_entries + group - 1) // group, score, 0)

    def add(it, _):
        found = []
        for g in range(group):
            k = it * group + g
            sb, j = pairs[k] // meta.blocks, pairs[k] % meta.blocks
            c = meta.count(member, flags, sb // meta.groups, sb, j).astype(jnp.float32)
            value = jnp.sum(jnp.exp(z_ref[sb, j] - peak[pl.ds(sb, 1), :]), axis=0, keepdims=True)
            found.append((sb, jnp.where(k < n_pairs, value * c, 0.0)))
        for sb, value in found:
            total[pl.ds(sb, 1), :] += value
        return 0

    lax.fori_loop(0, (n_pairs + group - 1) // group, add, 0)
    sums = total[...]
    lse_ref[...] = jnp.where(sums > 0, peak[...] + jnp.log(jnp.maximum(sums, 1e-30)), LOW)


def grad_kernel(meta, first, width, member, z_ref, q_ref, lse_ref, dep, out_ref, todo):
    def block(i, _):
        j = first + i
        n = 0
        for sb in range(meta.rows):
            todo[n] = sb
            n = n + member[sb, j]
        for g in range(width):
            todo[n + g] = 0
        at = pl.ds(pl.multiple_of(i * BLK, BLK), BLK)
        out_ref[at, :] = jnp.zeros((BLK, out_ref.shape[1]), jnp.float32)

        def step(it, _):
            his, los, rows = [], [], []
            for g in range(width):
                k = it * width + g
                sb = todo[k]
                p = jnp.exp(z_ref[sb, j] - lse_ref[pl.ds(sb, 1), :])
                hi, lo = split(jnp.where(k < n, p, 0.0))
                his.append(hi)
                los.append(lo)
                rows.append(q_ref[sb])
            left = jnp.concatenate([jnp.concatenate(his, axis=1), jnp.concatenate(los, axis=1)], axis=0)
            acc = dot(left, jnp.concatenate(rows, axis=0), 1, 0)
            out_ref[at, :] += acc[:BLK] + acc[BLK:]
            return 0

        lax.fori_loop(0, (n + width - 1) // width, step, 0)
        return 0

    lax.fori_loop(0, out_ref.shape[0] // BLK, block, 0)


def term_kernel(meta, spread, width, part, parts, member, owner, entries, z_ref, w_ref, lse_ref, pos_ref, dep, old, out_ref,
                flags, rows_ref):
    meta.flags(owner, flags)
    me = lax.axis_index("cache")
    below = lax.broadcasted_iota(jnp.int32, (BLK, BLK), 0)
    for s in range(meta.steps):
        for b in range(meta.groups):
            sb = s * meta.groups + b
            rows_ref[sb:sb + 1, :] = pos_ref[s:s + 1, b * BLK:(b + 1) * BLK]

    def clear(i, _):
        for s in range(meta.steps):
            out_ref[i, s] = jnp.zeros(out_ref.shape[2:], jnp.float32)
        return 0

    if part == 0:
        lax.fori_loop(0, meta.groups, clear, 0)
    n = entries[entries.shape[0] - 1]
    trips = (n + width - 1) // width

    def step(it, _):
        found = []
        for g in range(width):
            k = it * width + g
            j, both = entries[k] % meta.blocks, entries[k] // meta.blocks
            sbs = both // meta.rows, both % meta.rows
            s = sbs[0] // meta.groups
            hot = ((flags[s] > 0) & (j < meta.slab_blocks)).astype(jnp.float32)
            his, los = [], []
            for half, sb in enumerate(sbs):
                c = meta.count(member, flags, s, sb, j).astype(jnp.float32)
                p = jnp.exp(z_ref[sb, j] - lse_ref[pl.ds(sb, 1), :]) * c
                row = rows_ref[pl.ds(sb, 1), :] - j * BLK
                p = p - jnp.where(row == below, hot, 0.0)
                live = (k < n) if half == 0 else (k < n) & (sbs[1] != sbs[0])
                hi, lo = split(jnp.where(live, p, 0.0).T)
                his.append(hi)
                los.append(lo)
            hi = jnp.concatenate(his, axis=0)
            w = w_ref[meta.source(flags, s, j)]
            acc = dot(jnp.concatenate([hi, hi], axis=1), w, 1, 0) + dot(jnp.concatenate(los, axis=0), w[:BLK], 1, 0)
            found.append((s, sbs, acc))
        for s, sbs, acc in found:
            for half, sb in enumerate(sbs):
                place = sb - s * meta.groups
                if spread:
                    r = me ^ place
                    place = r // 2 + jnp.where(r % 2 == 1, 0, meta.groups // 2)
                out_ref[place, s] += acc[half * BLK:(half + 1) * BLK]
        return 0

    lax.fori_loop(trips * part // parts, trips * (part + 1) // parts, step, 0)


def params(mib):
    return pltpu.CompilerParams(vmem_limit_bytes=mib * 1024 * 1024)


def free():
    return pl.CostEstimate(flops=0, bytes_accessed=0, transcendentals=0)


SMEM = pl.BlockSpec(memory_space=pltpu.SMEM)
VMEM = pl.BlockSpec(memory_space=pltpu.VMEM)
ANY = pl.BlockSpec(memory_space=pl.ANY)
HBM = pl.BlockSpec(memory_space=pltpu.HBM)


def run_scores(meta, member, owner, queries, cache, fresh):
    width = cache.shape[1]
    group = 4
    n_src = meta.blocks + meta.slab_blocks
    most = meta.steps * meta.blocks * ((meta.groups + 1) // 2)
    return pl.pallas_call(
        functools.partial(scores_kernel, meta, group, 2.0 / math.sqrt(width)),
        in_specs=[SMEM, SMEM, HBM, HBM, HBM],
        out_specs=[VMEM] * 4 + [SMEM],
        out_shape=[
            pltpu.VMEM((meta.rows, meta.blocks, BLK, BLK), jnp.float32),
            pltpu.VMEM((n_src, 2 * BLK, width), jnp.bfloat16),
            pltpu.VMEM((meta.rows, BLK, width), jnp.bfloat16),
            pltpu.VMEM((meta.rows, BLK), jnp.float32),
            jax.ShapeDtypeStruct((most + group + 2,), jnp.int32),
        ],
        scratch_shapes=[
            pltpu.VMEM(cache.shape, jnp.float32),
            pltpu.VMEM(fresh.shape, jnp.float32),
            pltpu.VMEM((meta.rows, BLK), jnp.float32),
            pltpu.VMEM((meta.rows, BLK), jnp.float32),
            pltpu.SMEM((2 * meta.steps,), jnp.int32),
            pltpu.SMEM((meta.size + group,), jnp.int32),
            pltpu.SemaphoreType.DMA((3,)),
        ],
        compiler_params=params(20),
        name="scores",
    )(member, owner, *(pltpu.with_memory_space_constraint(x, pltpu.HBM)
                       for x in (queries.reshape(meta.rows, BLK, width), cache, fresh)))


def run_grads(meta, member, z, q, lse, first, count, dep):
    group = 4
    return pl.pallas_call(
        functools.partial(grad_kernel, meta, first, group),
        in_specs=[SMEM, VMEM, VMEM, VMEM, ANY],
        out_specs=VMEM,
        out_shape=pltpu.VMEM((count * BLK, q.shape[2]), jnp.float32),
        scratch_shapes=[pltpu.SMEM((meta.rows + group,), jnp.int32)],
        compiler_params=params(10),
        cost_estimate=free(),
        name="cache_grad",
    )(member, z, q, lse, dep)


def run_terms(meta, member, owner, entries, z, w, lse, pos, spread, dep, part=0, parts=1, old=None):
    group = 3
    return pl.pallas_call(
        functools.partial(term_kernel, meta, spread, group, part, parts),
        in_specs=[SMEM, SMEM, SMEM, VMEM, VMEM, VMEM, VMEM, ANY, VMEM if part else ANY],
        input_output_aliases={8: 0} if part else {},
        out_specs=VMEM,
        out_shape=pltpu.VMEM((meta.groups, meta.steps, BLK, w.shape[2]), jnp.float32),
        scratch_shapes=[pltpu.SMEM((2 * meta.steps,), jnp.int32), pltpu.VMEM((meta.rows, BLK), jnp.int32)],
        compiler_params=params(10),
        cost_estimate=free(),
        name="query_term",
    )(member, owner, entries, z, w, lse, pos, dep, old if part else dep)


def small(kernel, inputs, n_deps, outs, name, aliases=None, flops=0):
    n_vmem = len(inputs) - n_deps
    return pl.pallas_call(
        kernel,
        in_specs=[VMEM] * n_vmem + [ANY] * n_deps,
        out_specs=[VMEM] * len(outs),
        out_shape=[pltpu.VMEM(shape, jnp.float32) for shape in outs],
        input_output_aliases=aliases or {},
        compiler_params=params(4),
        cost_estimate=pl.CostEstimate(flops=flops, bytes_accessed=0, transcendentals=0),
        name=name,
    )(*inputs)


def merge_kernel(*refs):
    xs, out_ref = [r[...] for r in refs[:-1]], refs[-1]
    top = functools.reduce(jnp.maximum, xs)
    out_ref[...] = top + jnp.log(sum(jnp.exp(x - top) for x in xs))


def exchange_lse(lse):
    n = lax.axis_size("cache")
    bits = [1 << i for i in range(n.bit_length() - 1)]
    rounds = [bits[:1]] + [bits[i:i + 2] for i in range(1, len(bits), 2)]
    for some in rounds:
        partners = some if len(some) == 1 else [some[0], some[1], some[0] | some[1]]
        got = [lax.ppermute(lse, "cache", [(i, i ^ p) for i in range(n)]) for p in partners]
        lse = small(merge_kernel, [lse] + got, 0, [lse.shape], "merge_lse")[0]
    return lse


class Line:
    def __init__(self, n, rows, width):
        self.n, self.rows, self.width = n, rows, width
        self.lag_in, self.lag_mid, self.lag_out = LAGS
        self.late = self.lag_in + self.lag_mid
        self.slots = n + self.late + self.lag_out
        self.swap, self.mid, self.inner, self.total = {}, {}, {}, {}
        self.out = None

    def begin(self, array):
        self.swap[0] = lax.ppermute(array, "batch", [(0, 1), (1, 0), (2, 3), (3, 2)])

    def slot(self, t, chunk, deps):
        n, rows = self.n, self.rows
        u, k, o = t - self.lag_in, t - self.late, t - self.late - self.lag_out
        inputs, plan, outs = [], [], []

        def take(x):
            inputs.append(x)
            return len(inputs) - 1

        def give(shape=(rows, self.width)):
            outs.append(shape)
            return len(outs) - 1

        aliases = {}
        if 0 <= u < n:
            array, first = chunk(u)
            came, row = (self.swap[0], u * rows) if u < self.lag_in else (self.swap[u], 0)
            plan.append(("in", take(array), first, take(came), row, give()))
        if 0 <= k < n:
            plan.append(("sum", take(self.inner[k]), take(self.mid[k]), give()))
        if t < n:
            array, first = chunk(t)
            plan.append(("away", take(array), first, give()))
        if 0 <= o < n:
            args = take(self.total[o]), take(self.swap[o + self.late])
            old = None if self.out is None else take(self.out)
            new = give((n * rows, self.width))
            if old is not None:
                aliases = {old: new}
            plan.append(("out",) + args + (new,))
        n_in = len(inputs)

        def kernel(*refs):
            at = lax.axis_index("batch")
            end = (at == 0) | (at == 3)
            res = refs[n_in + len(deps):]
            total = None
            for what, *a in plan:
                if what == "in":
                    res[a[4]][...] = refs[a[0]][a[1]:a[1] + rows, :] + refs[a[2]][a[3]:a[3] + rows, :]
                elif what == "sum":
                    total = refs[a[0]][...] + refs[a[1]][...]
                    res[a[2]][...] = total
                elif what == "away":
                    value = refs[a[0]][a[1]:a[1] + rows, :]
                    res[a[2]][...] = value if total is None else jnp.where(end, value, total)
                else:
                    res[a[2]][o * rows:(o + 1) * rows, :] = jnp.where(end, refs[a[1]][...], refs[a[0]][...])

        got = small(kernel, inputs + list(deps), len(deps), outs, "line_slot", aliases, SLOT_FLOPS)
        away = None
        for what, *a in plan:
            if what == "in":
                self.inner[u] = got[a[4]]
            elif what == "sum":
                away = self.total[k] = got[a[2]]
            elif what == "away":
                away = got[a[2]]
            else:
                self.out = got[a[2]]
        if away is not None:
            self.swap[t] = lax.ppermute(away, "batch", [(0, 1), (1, 0), (2, 3), (3, 2)])
        if 0 <= u < n:
            self.mid[u] = lax.ppermute(self.inner[u], "batch", [(1, 2), (2, 1)])
        return got[0]


class HomeSum:
    def __init__(self, terms):
        self.n = lax.axis_size("cache")
        self.terms = terms
        self.steps, self.rows, self.width = terms.shape[1:]
        self.bits = [1 << i for i in range(1, self.n.bit_length() - 1)]
        self.stage = 0

    def move(self, x, bit):
        return lax.ppermute(x, "cache", [(i, i ^ bit) for i in range(self.n)])

    def start(self, dep):
        def kernel(terms, dep, odd):
            def one(i, _):
                for s in range(odd.shape[1]):
                    odd[i, s] = terms[i, s]
                return 0

            lax.fori_loop(0, odd.shape[0], one, 0)

        odd = small(kernel, [self.terms, dep], 1, [(self.n // 2,) + self.terms.shape[1:]], "home_start")[0]
        self.got = self.move(odd, 1)

    def step(self, dep):
        half = self.rows // 2
        orders = (self.bits, self.bits[::-1])
        last = self.stage == len(self.bits)
        if self.stage == 0:
            inputs = [self.terms, self.got]
            sources = [({2 * i: i for i in range(self.n // 2)}, 0, 1, h * half) for h in (0, 1)]
        else:
            inputs, sources = [], []
            for (place, keep), got in zip(self.kept, self.moved):
                sources.append((place, len(inputs), len(inputs) + 1, 0))
                inputs += [keep, got]
        writes, outs, kept = [], [], []
        for h, (place, a, b, first) in enumerate(sources):
            if last:
                writes.append((h, 0, 0, h * half))
                continue
            bit = orders[h][self.stage]
            far = [r for r in sorted(place) if r & bit]
            near = [r for r in sorted(place) if not r & bit]
            for rs in (far, near):
                outs.append((len(rs), self.steps, half, self.width))
                writes += [(h, r, (len(outs) - 1, i), None) for i, r in enumerate(rs)]
            kept.append({r: i for i, r in enumerate(near)})
        if last:
            outs = [(self.steps, self.rows, self.width)]
        n_in, steps = len(inputs), self.steps
        skip = self.n // 2 if self.stage == 0 else 0

        def kernel(*refs):
            res = refs[n_in + 1:]
            for h, r, to, at in writes:
                place, a, b, first = sources[h]
                i = place[r]

                def one(s, _, a=a, b=b, i=i, first=first, to=to, at=at):
                    value = refs[a][skip + i, s, first:first + half, :] + refs[b][i, s, first:first + half, :]
                    if at is None:
                        res[to[0]][to[1], s] = value
                    else:
                        res[0][s, at:at + half, :] = value
                    return 0

                lax.fori_loop(0, steps, one, 0)

        got = small(kernel, inputs + [dep], 1, outs, "home_sum")
        if last:
            return got[0]
        self.kept = [(kept[h], got[2 * h + 1]) for h in (0, 1)]
        self.moved = [self.move(got[2 * h], orders[h][self.stage]) for h in (0, 1)]
        self.stage += 1
        return got[1]


def on_device(queries, positives, block_list, block_count, refresh_owner, cache, fresh):
    steps, group_rows, width = queries.shape
    groups = group_rows // BLK
    blocks, slab_blocks = cache.shape[0] // BLK, fresh.shape[0] // BLK
    meta = Meta(steps, groups, blocks, slab_blocks)
    me = lax.axis_index("cache")
    block_ids = me * blocks + jnp.arange(blocks, dtype=jnp.int32)
    valid = jnp.arange(block_list.shape[2], dtype=jnp.int32)[None, None, :] < block_count[:, :, None]
    member = jnp.any((block_list[..., None] == block_ids) & valid[..., None], axis=2)
    member = member.astype(jnp.int32).reshape(meta.rows, blocks)
    owner = refresh_owner.astype(jnp.int32)

    z, w, q, own_lse, entries = run_scores(meta, member, owner, queries, cache, fresh)
    lse = exchange_lse(own_lse)

    half = BLK // 2
    early = min(LAGS[0] * half // BLK, blocks)
    grads = [run_grads(meta, member, z, q, lse, 0, early, lse)]
    owners = lax.axis_size("cache")
    share = group_rows // owners
    fast = share == BLK and owners == groups and owners & (owners - 1) == 0 and owners > 2
    home = mine = None

    def chunk(k):
        n = early * BLK // half
        return (grads[0], k * half) if k < n else (grads[1], (k - n) * half)

    def rest(dep):
        grads.append(run_grads(meta, member, z, q, lse, early, blocks - early, dep))
        if not fast:
            return grads[1], None
        terms = run_terms(meta, member, owner, entries, z, w, lse, positives, True, grads[1], 0, PARTS)
        return terms, HomeSum(terms)

    def more(part, dep):
        home.terms = run_terms(meta, member, owner, entries, z, w, lse, positives, True, dep, part, PARTS, home.terms)
        return home.terms

    if lax.axis_size("batch") == 4 and blocks > early:
        line = Line(2 * blocks, half, width)
        line.begin(grads[0])
        dep, home = rest(grads[0])
        deps = [dep]
        for t in range(LAGS[0], line.slots):
            deps = [line.slot(t, chunk, deps)]
            if fast and t in TERM_SLOTS:
                deps.append(more(1 + TERM_SLOTS.index(t), deps[0]))
            if fast and t == START_SLOT:
                home.start(deps[0])
            if fast and t in HOME_SLOTS:
                deps.append(home.step(deps[0]))
                mine = deps[-1]
        grad = line.out
    else:
        _, home = rest(lse)
        if fast:
            for part in range(1, PARTS):
                more(part, lse)
            home.start(lse)
        grad = lax.psum(jnp.concatenate(grads, axis=0), "batch")
    if fast:
        while home.stage < len(home.bits):
            home.step(lse)
        if mine is None or mine.ndim != 3:
            mine = home.step(lse)
    else:
        term = run_terms(meta, member, owner, entries, z, w, lse, positives, False, lse)
        term = jnp.swapaxes(term, 0, 1).reshape(steps, group_rows, width)
        mine = lax.psum_scatter(term, "cache", scatter_dimension=1, tiled=True)
    return mine, grad


def solution(mesh):
    return jax.shard_map(
        on_device,
        mesh=mesh,
        in_specs=(
            P(None, "batch", None),
            P(None, "batch"),
            P(None, "batch", None),
            P(None, "batch"),
            P(),
            P("cache", None),
            P("cache", None),
        ),
        out_specs=(P(None, ("batch", "cache"), None), P("cache", None)),
        check_vma=False,
    )
```

```python
import functools
import math

import jax
import jax.numpy as jnp
from jax import lax
from jax.experimental import pallas as pl
from jax.experimental.pallas import tpu as pltpu
from jax.sharding import PartitionSpec as P

BLK = 128
LOW = -1e30
LAGS = (4, 2, 2)
HOME_SLOTS = (9, 17, 21)
START_SLOT = 6
SLOT_FLOPS = 4_000_000_000


def dot(a, b, ca, cb):
    return lax.dot_general(a, b, (((ca,), (cb,)), ((), ())), preferred_element_type=jnp.float32)


def split(x):
    hi = x.astype(jnp.bfloat16)
    return hi, (x - hi.astype(jnp.float32)).astype(jnp.bfloat16)


class Meta:
    def __init__(self, steps, groups, blocks, slab_blocks):
        self.steps, self.groups, self.blocks, self.slab_blocks = steps, groups, blocks, slab_blocks
        self.rows = steps * groups
        self.size = self.rows * blocks

    def flags(self, owner, out):
        me = lax.axis_index("cache")
        seen = 0
        for s in range(self.steps):
            own = (owner[s] == me).astype(jnp.int32)
            seen = jnp.maximum(seen, own)
            out[s] = own
            out[self.steps + s] = seen

    def count(self, member, flags, s, sb, j):
        return member[sb, j] + jnp.where(j < self.slab_blocks, flags[s], 0)

    def source(self, flags, s, j):
        return jnp.where((flags[self.steps + s] > 0) & (j < self.slab_blocks), self.blocks + j, j)


def scores_kernel(meta, group, scale, member, owner, q_hbm, cache_hbm, fresh_hbm, z_ref, w_ref, q_ref, lse_ref, entries,
                  cache_ref, fresh_ref, peak, total, flags, pairs, sem):
    copies = [pltpu.make_async_copy(src, dst, sem.at[i]) for i, (src, dst) in enumerate(
        ((cache_hbm, cache_ref), (fresh_hbm, fresh_ref), (q_hbm, q_ref)))]
    for copy in copies:
        copy.start()
    meta.flags(owner, flags)

    def collect(sj, carry):
        n_entries, n_pairs = carry
        s, j = sj // meta.blocks, sj % meta.blocks
        m, held = 0, 0
        for b in range(meta.groups):
            sb = s * meta.groups + b
            on = (meta.count(member, flags, s, sb, j) > 0).astype(jnp.int32)
            pairs[n_pairs] = sb * meta.blocks + j
            n_pairs = n_pairs + on
            held = jnp.where(m % 2 == 0, sb, held)
            entries[n_entries + m // 2] = (held * meta.rows + sb) * meta.blocks + j
            m = m + on

        @pl.when(m % 2 == 1)
        def _():
            entries[n_entries + m // 2] = (held * meta.rows + held) * meta.blocks + j

        return n_entries + (m + 1) // 2, n_pairs

    n_entries, n_pairs = lax.fori_loop(0, meta.steps * meta.blocks, collect, (0, 0))
    for g in range(group):
        entries[n_entries + g] = jnp.where(n_entries > 0, entries[0], 0)
        pairs[n_pairs + g] = 0
    entries[entries.shape[0] - 1] = n_entries
    peak[...] = jnp.full(peak.shape, LOW, jnp.float32)
    total[...] = jnp.zeros(total.shape, jnp.float32)

    for copy, src, at in ((copies[0], cache_ref, 0), (copies[1], fresh_ref, meta.blocks)):
        copy.wait()

        def one(k, _, src=src, at=at):
            hi, lo = split(src[pl.ds(pl.multiple_of(k * BLK, BLK), BLK), :])
            w_ref[at + k, :BLK] = hi
            w_ref[at + k, BLK:] = lo
            return 0

        lax.fori_loop(0, src.shape[0] // BLK, one, 0)
    copies[2].wait()

    def score(it, _):
        found = []
        for g in range(group):
            e = entries[it * group + g]
            j, both = e % meta.blocks, e // meta.blocks
            sb0, sb1 = both // meta.rows, both % meta.rows
            right = jnp.concatenate([q_ref[sb0], q_ref[sb1]], axis=0)
            z = dot(w_ref[meta.source(flags, sb0 // meta.groups, j)], right, 1, 1)
            found.append((sb0, sb1, j, (z[:BLK] + z[BLK:]) * scale))
        for sb0, sb1, j, z in found:
            for sb, one in ((sb0, z[:, :BLK]), (sb1, z[:, BLK:])):
                z_ref[sb, j] = one
                row = pl.ds(sb, 1)
                peak[row, :] = jnp.maximum(peak[row, :], jnp.max(one, axis=0, keepdims=True))
        return 0

    lax.fori_loop(0, (n_entries + group - 1) // group, score, 0)

    def add(it, _):
        found = []
        for g in range(group):
            k = it * group + g
            sb, j = pairs[k] // meta.blocks, pairs[k] % meta.blocks
            c = meta.count(member, flags, sb // meta.groups, sb, j).astype(jnp.float32)
            value = jnp.sum(jnp.exp(z_ref[sb, j] - peak[pl.ds(sb, 1), :]), axis=0, keepdims=True)
            found.append((sb, jnp.where(k < n_pairs, value * c, 0.0)))
        for sb, value in found:
            total[pl.ds(sb, 1), :] += value
        return 0

    lax.fori_loop(0, (n_pairs + group - 1) // group, add, 0)
    sums = total[...]
    lse_ref[...] = jnp.where(sums > 0, peak[...] + jnp.log(jnp.maximum(sums, 1e-30)), LOW)


def grad_kernel(meta, first, width, member, z_ref, q_ref, lse_ref, dep, out_ref, todo):
    def block(i, _):
        j = first + i
        n = 0
        for sb in range(meta.rows):
            todo[n] = sb
            n = n + member[sb, j]
        for g in range(width):
            todo[n + g] = 0
        at = pl.ds(pl.multiple_of(i * BLK, BLK), BLK)
        out_ref[at, :] = jnp.zeros((BLK, out_ref.shape[1]), jnp.float32)

        def step(it, _):
            his, los, rows = [], [], []
            for g in range(width):
                k = it * width + g
                sb = todo[k]
                p = jnp.exp(z_ref[sb, j] - lse_ref[pl.ds(sb, 1), :])
                hi, lo = split(jnp.where(k < n, p, 0.0))
                his.append(hi)
                los.append(lo)
                rows.append(q_ref[sb])
            left = jnp.concatenate([jnp.concatenate(his, axis=1), jnp.concatenate(los, axis=1)], axis=0)
            acc = dot(left, jnp.concatenate(rows, axis=0), 1, 0)
            out_ref[at, :] += acc[:BLK] + acc[BLK:]
            return 0

        lax.fori_loop(0, (n + width - 1) // width, step, 0)
        return 0

    lax.fori_loop(0, out_ref.shape[0] // BLK, block, 0)


def term_kernel(meta, spread, width, member, owner, entries, z_ref, w_ref, lse_ref, pos_ref, dep, out_ref, flags, rows_ref):
    meta.flags(owner, flags)
    me = lax.axis_index("cache")
    below = lax.broadcasted_iota(jnp.int32, (BLK, BLK), 0)
    for s in range(meta.steps):
        for b in range(meta.groups):
            sb = s * meta.groups + b
            rows_ref[sb:sb + 1, :] = pos_ref[s:s + 1, b * BLK:(b + 1) * BLK]

    def clear(i, _):
        for s in range(meta.steps):
            out_ref[i, s] = jnp.zeros(out_ref.shape[2:], jnp.float32)
        return 0

    lax.fori_loop(0, meta.groups, clear, 0)
    n = entries[entries.shape[0] - 1]

    def step(it, _):
        found = []
        for g in range(width):
            k = it * width + g
            j, both = entries[k] % meta.blocks, entries[k] // meta.blocks
            sbs = both // meta.rows, both % meta.rows
            s = sbs[0] // meta.groups
            hot = ((flags[s] > 0) & (j < meta.slab_blocks)).astype(jnp.float32)
            his, los = [], []
            for half, sb in enumerate(sbs):
                c = meta.count(member, flags, s, sb, j).astype(jnp.float32)
                p = jnp.exp(z_ref[sb, j] - lse_ref[pl.ds(sb, 1), :]) * c
                row = rows_ref[pl.ds(sb, 1), :] - j * BLK
                p = p - jnp.where(row == below, hot, 0.0)
                live = (k < n) if half == 0 else (k < n) & (sbs[1] != sbs[0])
                hi, lo = split(jnp.where(live, p, 0.0).T)
                his.append(hi)
                los.append(lo)
            hi = jnp.concatenate(his, axis=0)
            w = w_ref[meta.source(flags, s, j)]
            acc = dot(jnp.concatenate([hi, hi], axis=1), w, 1, 0) + dot(jnp.concatenate(los, axis=0), w[:BLK], 1, 0)
            found.append((s, sbs, acc))
        for s, sbs, acc in found:
            for half, sb in enumerate(sbs):
                place = sb - s * meta.groups
                if spread:
                    r = me ^ place
                    place = r // 2 + jnp.where(r % 2 == 1, 0, meta.groups // 2)
                out_ref[place, s] += acc[half * BLK:(half + 1) * BLK]
        return 0

    lax.fori_loop(0, (n + width - 1) // width, step, 0)


def params(mib):
    return pltpu.CompilerParams(vmem_limit_bytes=mib * 1024 * 1024)


def free():
    return pl.CostEstimate(flops=0, bytes_accessed=0, transcendentals=0)


SMEM = pl.BlockSpec(memory_space=pltpu.SMEM)
VMEM = pl.BlockSpec(memory_space=pltpu.VMEM)
ANY = pl.BlockSpec(memory_space=pl.ANY)
HBM = pl.BlockSpec(memory_space=pltpu.HBM)


def run_scores(meta, member, owner, queries, cache, fresh):
    width = cache.shape[1]
    group = 4
    n_src = meta.blocks + meta.slab_blocks
    most = meta.steps * meta.blocks * ((meta.groups + 1) // 2)
    return pl.pallas_call(
        functools.partial(scores_kernel, meta, group, 2.0 / math.sqrt(width)),
        in_specs=[SMEM, SMEM, HBM, HBM, HBM],
        out_specs=[VMEM] * 4 + [SMEM],
        out_shape=[
            pltpu.VMEM((meta.rows, meta.blocks, BLK, BLK), jnp.float32),
            pltpu.VMEM((n_src, 2 * BLK, width), jnp.bfloat16),
            pltpu.VMEM((meta.rows, BLK, width), jnp.bfloat16),
            pltpu.VMEM((meta.rows, BLK), jnp.float32),
            jax.ShapeDtypeStruct((most + group + 2,), jnp.int32),
        ],
        scratch_shapes=[
            pltpu.VMEM(cache.shape, jnp.float32),
            pltpu.VMEM(fresh.shape, jnp.float32),
            pltpu.VMEM((meta.rows, BLK), jnp.float32),
            pltpu.VMEM((meta.rows, BLK), jnp.float32),
            pltpu.SMEM((2 * meta.steps,), jnp.int32),
            pltpu.SMEM((meta.size + group,), jnp.int32),
            pltpu.SemaphoreType.DMA((3,)),
        ],
        compiler_params=params(20),
        name="scores",
    )(member, owner, *(pltpu.with_memory_space_constraint(x, pltpu.HBM)
                       for x in (queries.reshape(meta.rows, BLK, width), cache, fresh)))


def run_grads(meta, member, z, q, lse, first, count, dep):
    group = 4
    return pl.pallas_call(
        functools.partial(grad_kernel, meta, first, group),
        in_specs=[SMEM, VMEM, VMEM, VMEM, ANY],
        out_specs=VMEM,
        out_shape=pltpu.VMEM((count * BLK, q.shape[2]), jnp.float32),
        scratch_shapes=[pltpu.SMEM((meta.rows + group,), jnp.int32)],
        compiler_params=params(10),
        cost_estimate=free(),
        name="cache_grad",
    )(member, z, q, lse, dep)


def run_terms(meta, member, owner, entries, z, w, lse, pos, spread, dep):
    group = 3
    return pl.pallas_call(
        functools.partial(term_kernel, meta, spread, group),
        in_specs=[SMEM, SMEM, SMEM, VMEM, VMEM, VMEM, VMEM, ANY],
        out_specs=VMEM,
        out_shape=pltpu.VMEM((meta.groups, meta.steps, BLK, w.shape[2]), jnp.float32),
        scratch_shapes=[pltpu.SMEM((2 * meta.steps,), jnp.int32), pltpu.VMEM((meta.rows, BLK), jnp.int32)],
        compiler_params=params(10),
        cost_estimate=free(),
        name="query_term",
    )(member, owner, entries, z, w, lse, pos, dep)


def small(kernel, inputs, n_deps, outs, name, aliases=None, flops=0):
    n_vmem = len(inputs) - n_deps
    return pl.pallas_call(
        kernel,
        in_specs=[VMEM] * n_vmem + [ANY] * n_deps,
        out_specs=[VMEM] * len(outs),
        out_shape=[pltpu.VMEM(shape, jnp.float32) for shape in outs],
        input_output_aliases=aliases or {},
        compiler_params=params(4),
        cost_estimate=pl.CostEstimate(flops=flops, bytes_accessed=0, transcendentals=0),
        name=name,
    )(*inputs)


def merge_kernel(*refs):
    xs, out_ref = [r[...] for r in refs[:-1]], refs[-1]
    top = functools.reduce(jnp.maximum, xs)
    out_ref[...] = top + jnp.log(sum(jnp.exp(x - top) for x in xs))


def exchange_lse(lse):
    n = lax.axis_size("cache")
    bits = [1 << i for i in range(n.bit_length() - 1)]
    rounds = [bits[:1]] + [bits[i:i + 2] for i in range(1, len(bits), 2)]
    for some in rounds:
        partners = some if len(some) == 1 else [some[0], some[1], some[0] | some[1]]
        got = [lax.ppermute(lse, "cache", [(i, i ^ p) for i in range(n)]) for p in partners]
        lse = small(merge_kernel, [lse] + got, 0, [lse.shape], "merge_lse")[0]
    return lse


class Line:
    def __init__(self, n, rows, width):
        self.n, self.rows, self.width = n, rows, width
        self.lag_in, self.lag_mid, self.lag_out = LAGS
        self.late = self.lag_in + self.lag_mid
        self.slots = n + self.late + self.lag_out
        self.swap, self.mid, self.inner, self.total = {}, {}, {}, {}
        self.out = None

    def swapped(self, array):
        return lax.ppermute(array, "batch", [(0, 1), (1, 0), (2, 3), (3, 2)])

    def swapped_mid(self, array):
        return lax.ppermute(array, "batch", [(1, 2), (2, 1)])

    def begin(self, array, more):
        self.swap_a, self.swap_b = self.swapped(array), self.swapped(more)

    def early(self, array, dep):
        def kernel(own, came, dep, out):
            out[...] = own[...] + came[...]

        self.inner_a = small(kernel, [array, self.swap_a, dep], 1, [array.shape], "line_early")[0]
        self.mid_a = self.swapped_mid(self.inner_a)
        return self.inner_a

    def slot(self, t, chunk, deps):
        n, rows = self.n, self.rows
        u, k, o = t - self.lag_in, t - self.late, t - self.late - self.lag_out
        inputs, plan, outs = [], [], []

        def take(x):
            inputs.append(x)
            return len(inputs) - 1

        def give(shape=(rows, self.width)):
            outs.append(shape)
            return len(outs) - 1

        aliases = {}
        if 0 <= u < n:
            array, first = chunk(u)
            came, row = (self.swap_b, (u - self.lag_mid) * rows) if u < self.late else (self.swap[u], 0)
            plan.append(("in", take(array), first, take(came), row, give()))
        if 0 <= k < n:
            pair, row = ((self.inner_a, self.mid_a), k * rows) if k < self.lag_mid else ((self.inner[k], self.mid[k]), 0)
            plan.append(("sum", take(pair[0]), take(pair[1]), row, give()))
        if t < n:
            array, first = chunk(t)
            plan.append(("away", take(array), first, give()))
        if 0 <= o < n:
            args = take(self.total[o]), take(self.swap[o + self.late])
            old = None if self.out is None else take(self.out)
            new = give((n * rows, self.width))
            if old is not None:
                aliases = {old: new}
            plan.append(("out",) + args + (new,))
        n_in = len(inputs)

        def kernel(*refs):
            at = lax.axis_index("batch")
            end = (at == 0) | (at == 3)
            res = refs[n_in + len(deps):]
            total = None
            for what, *a in plan:
                if what == "in":
                    res[a[4]][...] = refs[a[0]][a[1]:a[1] + rows, :] + refs[a[2]][a[3]:a[3] + rows, :]
                elif what == "sum":
                    total = refs[a[0]][a[2]:a[2] + rows, :] + refs[a[1]][a[2]:a[2] + rows, :]
                    res[a[3]][...] = total
                elif what == "away":
                    value = refs[a[0]][a[1]:a[1] + rows, :]
                    res[a[2]][...] = value if total is None else jnp.where(end, value, total)
                else:
                    res[a[2]][o * rows:(o + 1) * rows, :] = jnp.where(end, refs[a[1]][...], refs[a[0]][...])

        got = small(kernel, inputs + list(deps), len(deps), outs, "line_slot", aliases, SLOT_FLOPS)
        away = None
        for what, *a in plan:
            if what == "in":
                self.inner[u] = got[a[4]]
            elif what == "sum":
                away = self.total[k] = got[a[3]]
            elif what == "away":
                away = got[a[2]]
            else:
                self.out = got[a[2]]
        if away is not None:
            self.swap[t] = self.swapped(away)
        if 0 <= u < n:
            self.mid[u] = self.swapped_mid(self.inner[u])
        return got[0]


class HomeSum:
    def __init__(self, terms):
        self.n = lax.axis_size("cache")
        self.terms = terms
        self.steps, self.rows, self.width = terms.shape[1:]
        self.bits = [1 << i for i in range(1, self.n.bit_length() - 1)]
        self.stage = 0

    def move(self, x, bit):
        return lax.ppermute(x, "cache", [(i, i ^ bit) for i in range(self.n)])

    def start(self, dep):
        def kernel(terms, dep, odd):
            def one(i, _):
                for s in range(odd.shape[1]):
                    odd[i, s] = terms[i, s]
                return 0

            lax.fori_loop(0, odd.shape[0], one, 0)

        odd = small(kernel, [self.terms, dep], 1, [(self.n // 2,) + self.terms.shape[1:]], "home_start")[0]
        self.got = self.move(odd, 1)

    def step(self, dep):
        half = self.rows // 2
        orders = (self.bits, self.bits[::-1])
        last = self.stage == len(self.bits)
        if self.stage == 0:
            inputs = [self.terms, self.got]
            sources = [({2 * i: i for i in range(self.n // 2)}, 0, 1, h * half) for h in (0, 1)]
        else:
            inputs, sources = [], []
            for (place, keep), got in zip(self.kept, self.moved):
                sources.append((place, len(inputs), len(inputs) + 1, 0))
                inputs += [keep, got]
        writes, outs, kept = [], [], []
        for h, (place, a, b, first) in enumerate(sources):
            if last:
                writes.append((h, 0, 0, h * half))
                continue
            bit = orders[h][self.stage]
            far = [r for r in sorted(place) if r & bit]
            near = [r for r in sorted(place) if not r & bit]
            for rs in (far, near):
                outs.append((len(rs), self.steps, half, self.width))
                writes += [(h, r, (len(outs) - 1, i), None) for i, r in enumerate(rs)]
            kept.append({r: i for i, r in enumerate(near)})
        if last:
            outs = [(self.steps, self.rows, self.width)]
        n_in, steps = len(inputs), self.steps
        skip = self.n // 2 if self.stage == 0 else 0

        def kernel(*refs):
            res = refs[n_in + 1:]
            for h, r, to, at in writes:
                place, a, b, first = sources[h]
                i = place[r]

                def one(s, _, a=a, b=b, i=i, first=first, to=to, at=at):
                    value = refs[a][skip + i, s, first:first + half, :] + refs[b][i, s, first:first + half, :]
                    if at is None:
                        res[to[0]][to[1], s] = value
                    else:
                        res[0][s, at:at + half, :] = value
                    return 0

                lax.fori_loop(0, steps, one, 0)

        got = small(kernel, inputs + [dep], 1, outs, "home_sum")
        if last:
            return got[0]
        self.kept = [(kept[h], got[2 * h + 1]) for h in (0, 1)]
        self.moved = [self.move(got[2 * h], orders[h][self.stage]) for h in (0, 1)]
        self.stage += 1
        return got[1]


def on_device(queries, positives, block_list, block_count, refresh_owner, cache, fresh):
    steps, group_rows, width = queries.shape
    groups = group_rows // BLK
    blocks, slab_blocks = cache.shape[0] // BLK, fresh.shape[0] // BLK
    meta = Meta(steps, groups, blocks, slab_blocks)
    me = lax.axis_index("cache")
    block_ids = me * blocks + jnp.arange(blocks, dtype=jnp.int32)
    valid = jnp.arange(block_list.shape[2], dtype=jnp.int32)[None, None, :] < block_count[:, :, None]
    member = jnp.any((block_list[..., None] == block_ids) & valid[..., None], axis=2)
    member = member.astype(jnp.int32).reshape(meta.rows, blocks)
    owner = refresh_owner.astype(jnp.int32)

    z, w, q, own_lse, entries = run_scores(meta, member, owner, queries, cache, fresh)
    lse = exchange_lse(own_lse)

    half = BLK // 2
    line = Line(2 * blocks, half, width)
    parts = [line.lag_mid * half // BLK, line.lag_in * half // BLK]
    parts.append(max(blocks - sum(parts), 0))
    in_line = lax.axis_size("batch") == 4 and parts[2] > 0
    if not in_line:
        parts = [blocks]
    grads, dep = [], lse
    for i, part in enumerate(parts):
        grads.append(run_grads(meta, member, z, q, lse, sum(parts[:i]), part, dep))
        dep = grads[-1]
    owners = lax.axis_size("cache")
    share = group_rows // owners
    fast = share == BLK and owners == groups and owners & (owners - 1) == 0 and owners > 2
    home = mine = None

    def chunk(k):
        row = k * half
        for part, grad in zip(parts, grads):
            if row < part * BLK:
                return grad, row
            row -= part * BLK

    if in_line:
        line.begin(grads[0], grads[1])
        dep = line.early(grads[0], grads[2])
    if fast:
        dep = run_terms(meta, member, owner, entries, z, w, lse, positives, True, dep)
        home = HomeSum(dep)
    if in_line:
        deps = [dep]
        for t in range(line.late, line.slots):
            deps = [line.slot(t, chunk, deps)]
            if fast and t == START_SLOT:
                home.start(deps[0])
            if fast and t in HOME_SLOTS:
                deps.append(home.step(deps[0]))
                mine = deps[-1]
        grad = line.out
    else:
        grad = lax.psum(grads[0], "batch")
        if fast:
            home.start(lse)
    if fast:
        while home.stage < len(home.bits):
            home.step(lse)
        if mine is None or mine.ndim != 3:
            mine = home.step(lse)
    else:
        term = run_terms(meta, member, owner, entries, z, w, lse, positives, False, lse)
        term = jnp.swapaxes(term, 0, 1).reshape(steps, group_rows, width)
        mine = lax.psum_scatter(term, "cache", scatter_dimension=1, tiled=True)
    return mine, grad


def solution(mesh):
    return jax.shard_map(
        on_device,
        mesh=mesh,
        in_specs=(
            P(None, "batch", None),
            P(None, "batch"),
            P(None, "batch", None),
            P(None, "batch"),
            P(),
            P("cache", None),
            P("cache", None),
        ),
        out_specs=(P(None, ("batch", "cache"), None), P("cache", None)),
        check_vma=False,
    )
```

```python
import functools
import math

import jax
import jax.numpy as jnp
from jax import lax
from jax.experimental import pallas as pl
from jax.experimental.pallas import tpu as pltpu
from jax.sharding import PartitionSpec as P

BLK = 128
LOW = -1e30
LAGS = (4, 2, 2)
HOME_SLOTS = (11, 17, 21)
START_SLOT = 8
SLOT_FLOPS = 3_000_000_000


def dot(a, b, ca, cb):
    return lax.dot_general(a, b, (((ca,), (cb,)), ((), ())), preferred_element_type=jnp.float32)


def split(x):
    hi = x.astype(jnp.bfloat16)
    return hi, (x - hi.astype(jnp.float32)).astype(jnp.bfloat16)


class Meta:
    def __init__(self, steps, groups, blocks, slab_blocks):
        self.steps, self.groups, self.blocks, self.slab_blocks = steps, groups, blocks, slab_blocks
        self.rows = steps * groups
        self.size = self.rows * blocks

    def flags(self, owner, out):
        me = lax.axis_index("cache")
        seen = 0
        for s in range(self.steps):
            own = (owner[s] == me).astype(jnp.int32)
            seen = jnp.maximum(seen, own)
            out[s] = own
            out[self.steps + s] = seen

    def count(self, member, flags, s, sb, j):
        return member[sb, j] + jnp.where(j < self.slab_blocks, flags[s], 0)

    def source(self, flags, s, j):
        return jnp.where((flags[self.steps + s] > 0) & (j < self.slab_blocks), self.blocks + j, j)


def scores_kernel(meta, group, scale, member, owner, q_hbm, cache_hbm, fresh_hbm, z_ref, w_ref, q_ref, lse_ref, entries,
                  cache_ref, fresh_ref, peak, total, flags, pairs, sem):
    copies = [pltpu.make_async_copy(src, dst, sem.at[i]) for i, (src, dst) in enumerate(
        ((cache_hbm, cache_ref), (fresh_hbm, fresh_ref), (q_hbm, q_ref)))]
    for copy in copies:
        copy.start()
    meta.flags(owner, flags)

    def collect(sj, carry):
        n_entries, n_pairs = carry
        s, j = sj // meta.blocks, sj % meta.blocks
        m, held = 0, 0
        for b in range(meta.groups):
            sb = s * meta.groups + b
            on = (meta.count(member, flags, s, sb, j) > 0).astype(jnp.int32)
            pairs[n_pairs] = sb * meta.blocks + j
            n_pairs = n_pairs + on
            held = jnp.where(m % 2 == 0, sb, held)
            entries[n_entries + m // 2] = (held * meta.rows + sb) * meta.blocks + j
            m = m + on

        @pl.when(m % 2 == 1)
        def _():
            entries[n_entries + m // 2] = (held * meta.rows + held) * meta.blocks + j

        return n_entries + (m + 1) // 2, n_pairs

    n_entries, n_pairs = lax.fori_loop(0, meta.steps * meta.blocks, collect, (0, 0))
    for g in range(group):
        entries[n_entries + g] = jnp.where(n_entries > 0, entries[0], 0)
        pairs[n_pairs + g] = 0
    entries[entries.shape[0] - 1] = n_entries
    peak[...] = jnp.full(peak.shape, LOW, jnp.float32)
    total[...] = jnp.zeros(total.shape, jnp.float32)

    for copy, src, at in ((copies[0], cache_ref, 0), (copies[1], fresh_ref, meta.blocks)):
        copy.wait()

        def one(k, _, src=src, at=at):
            hi, lo = split(src[pl.ds(pl.multiple_of(k * BLK, BLK), BLK), :])
            w_ref[at + k, :BLK] = hi
            w_ref[at + k, BLK:] = lo
            return 0

        lax.fori_loop(0, src.shape[0] // BLK, one, 0)
    copies[2].wait()

    def score(it, _):
        found = []
        for g in range(group):
            e = entries[it * group + g]
            j, both = e % meta.blocks, e // meta.blocks
            sb0, sb1 = both // meta.rows, both % meta.rows
            right = jnp.concatenate([q_ref[sb0], q_ref[sb1]], axis=0)
            z = dot(w_ref[meta.source(flags, sb0 // meta.groups, j)], right, 1, 1)
            found.append((sb0, sb1, j, (z[:BLK] + z[BLK:]) * scale))
        for sb0, sb1, j, z in found:
            for sb, one in ((sb0, z[:, :BLK]), (sb1, z[:, BLK:])):
                z_ref[sb, j] = one
                row = pl.ds(sb, 1)
                peak[row, :] = jnp.maximum(peak[row, :], jnp.max(one, axis=0, keepdims=True))
        return 0

    lax.fori_loop(0, (n_entries + group - 1) // group, score, 0)

    def add(it, _):
        found = []
        for g in range(group):
            k = it * group + g
            sb, j = pairs[k] // meta.blocks, pairs[k] % meta.blocks
            c = meta.count(member, flags, sb // meta.groups, sb, j).astype(jnp.float32)
            value = jnp.sum(jnp.exp(z_ref[sb, j] - peak[pl.ds(sb, 1), :]), axis=0, keepdims=True)
            found.append((sb, jnp.where(k < n_pairs, value * c, 0.0)))
        for sb, value in found:
            total[pl.ds(sb, 1), :] += value
        return 0

    lax.fori_loop(0, (n_pairs + group - 1) // group, add, 0)
    sums = total[...]
    lse_ref[...] = jnp.where(sums > 0, peak[...] + jnp.log(jnp.maximum(sums, 1e-30)), LOW)


def grad_kernel(meta, first, width, member, z_ref, q_ref, lse_ref, dep, out_ref, todo):
    def block(i, _):
        j = first + i
        n = 0
        for sb in range(meta.rows):
            todo[n] = sb
            n = n + member[sb, j]
        for g in range(width):
            todo[n + g] = 0
        at = pl.ds(pl.multiple_of(i * BLK, BLK), BLK)
        out_ref[at, :] = jnp.zeros((BLK, out_ref.shape[1]), jnp.float32)

        def step(it, _):
            his, los, rows = [], [], []
            for g in range(width):
                k = it * width + g
                sb = todo[k]
                p = jnp.exp(z_ref[sb, j] - lse_ref[pl.ds(sb, 1), :])
                hi, lo = split(jnp.where(k < n, p, 0.0))
                his.append(hi)
                los.append(lo)
                rows.append(q_ref[sb])
            left = jnp.concatenate([jnp.concatenate(his, axis=1), jnp.concatenate(los, axis=1)], axis=0)
            acc = dot(left, jnp.concatenate(rows, axis=0), 1, 0)
            out_ref[at, :] += acc[:BLK] + acc[BLK:]
            return 0

        lax.fori_loop(0, (n + width - 1) // width, step, 0)
        return 0

    lax.fori_loop(0, out_ref.shape[0] // BLK, block, 0)


def term_kernel(meta, spread, width, part, parts, member, owner, entries, z_ref, w_ref, lse_ref, pos_ref, dep, *refs):
    out_ref, flags, rows_ref = refs[-3:]
    meta.flags(owner, flags)
    me = lax.axis_index("cache")
    below = lax.broadcasted_iota(jnp.int32, (BLK, BLK), 0)
    for s in range(meta.steps):
        for b in range(meta.groups):
            sb = s * meta.groups + b
            rows_ref[sb:sb + 1, :] = pos_ref[s:s + 1, b * BLK:(b + 1) * BLK]

    def clear(i, _):
        for s in range(meta.steps):
            out_ref[i, s] = jnp.zeros(out_ref.shape[2:], jnp.float32)
        return 0

    if part == 0:
        lax.fori_loop(0, meta.groups, clear, 0)
    n = entries[entries.shape[0] - 1]
    trips = (n + width - 1) // width

    def step(it, _):
        found = []
        for g in range(width):
            k = it * width + g
            j, both = entries[k] % meta.blocks, entries[k] // meta.blocks
            sbs = both // meta.rows, both % meta.rows
            s = sbs[0] // meta.groups
            hot = ((flags[s] > 0) & (j < meta.slab_blocks)).astype(jnp.float32)
            his, los = [], []
            for half, sb in enumerate(sbs):
                c = meta.count(member, flags, s, sb, j).astype(jnp.float32)
                p = jnp.exp(z_ref[sb, j] - lse_ref[pl.ds(sb, 1), :]) * c
                row = rows_ref[pl.ds(sb, 1), :] - j * BLK
                p = p - jnp.where(row == below, hot, 0.0)
                live = (k < n) if half == 0 else (k < n) & (sbs[1] != sbs[0])
                hi, lo = split(jnp.where(live, p, 0.0).T)
                his.append(hi)
                los.append(lo)
            hi = jnp.concatenate(his, axis=0)
            w = w_ref[meta.source(flags, s, j)]
            acc = dot(jnp.concatenate([hi, hi], axis=1), w, 1, 0) + dot(jnp.concatenate(los, axis=0), w[:BLK], 1, 0)
            found.append((s, sbs, acc))
        for s, sbs, acc in found:
            for half, sb in enumerate(sbs):
                place = sb - s * meta.groups
                if spread:
                    r = me ^ place
                    place = r // 2 + jnp.where(r % 2 == 1, 0, meta.groups // 2)
                out_ref[place, s] += acc[half * BLK:(half + 1) * BLK]
        return 0

    lax.fori_loop(trips * part // parts, trips * (part + 1) // parts, step, 0)


def params(mib):
    return pltpu.CompilerParams(vmem_limit_bytes=mib * 1024 * 1024)


def free():
    return pl.CostEstimate(flops=0, bytes_accessed=0, transcendentals=0)


SMEM = pl.BlockSpec(memory_space=pltpu.SMEM)
VMEM = pl.BlockSpec(memory_space=pltpu.VMEM)
ANY = pl.BlockSpec(memory_space=pl.ANY)
HBM = pl.BlockSpec(memory_space=pltpu.HBM)


def run_scores(meta, member, owner, queries, cache, fresh):
    width = cache.shape[1]
    group = 4
    n_src = meta.blocks + meta.slab_blocks
    most = meta.steps * meta.blocks * ((meta.groups + 1) // 2)
    return pl.pallas_call(
        functools.partial(scores_kernel, meta, group, 2.0 / math.sqrt(width)),
        in_specs=[SMEM, SMEM, HBM, HBM, HBM],
        out_specs=[VMEM] * 4 + [SMEM],
        out_shape=[
            pltpu.VMEM((meta.rows, meta.blocks, BLK, BLK), jnp.float32),
            pltpu.VMEM((n_src, 2 * BLK, width), jnp.bfloat16),
            pltpu.VMEM((meta.rows, BLK, width), jnp.bfloat16),
            pltpu.VMEM((meta.rows, BLK), jnp.float32),
            jax.ShapeDtypeStruct((most + group + 2,), jnp.int32),
        ],
        scratch_shapes=[
            pltpu.VMEM(cache.shape, jnp.float32),
            pltpu.VMEM(fresh.shape, jnp.float32),
            pltpu.VMEM((meta.rows, BLK), jnp.float32),
            pltpu.VMEM((meta.rows, BLK), jnp.float32),
            pltpu.SMEM((2 * meta.steps,), jnp.int32),
            pltpu.SMEM((meta.size + group,), jnp.int32),
            pltpu.SemaphoreType.DMA((3,)),
        ],
        compiler_params=params(20),
        name="scores",
    )(member, owner, *(pltpu.with_memory_space_constraint(x, pltpu.HBM)
                       for x in (queries.reshape(meta.rows, BLK, width), cache, fresh)))


def run_grads(meta, member, z, q, lse, first, count, dep):
    group = 4
    return pl.pallas_call(
        functools.partial(grad_kernel, meta, first, group),
        in_specs=[SMEM, VMEM, VMEM, VMEM, ANY],
        out_specs=VMEM,
        out_shape=pltpu.VMEM((count * BLK, q.shape[2]), jnp.float32),
        scratch_shapes=[pltpu.SMEM((meta.rows + group,), jnp.int32)],
        compiler_params=params(10),
        cost_estimate=free(),
        name="cache_grad",
    )(member, z, q, lse, dep)


def run_terms(meta, member, owner, entries, z, w, lse, pos, spread, dep, part=0, parts=1, old=None):
    group = 3
    return pl.pallas_call(
        functools.partial(term_kernel, meta, spread, group, part, parts),
        in_specs=[SMEM, SMEM, SMEM, VMEM, VMEM, VMEM, VMEM, ANY] + [VMEM] * (part > 0),
        input_output_aliases={8: 0} if part else {},
        out_specs=VMEM,
        out_shape=pltpu.VMEM((meta.groups, meta.steps, BLK, w.shape[2]), jnp.float32),
        scratch_shapes=[pltpu.SMEM((2 * meta.steps,), jnp.int32), pltpu.VMEM((meta.rows, BLK), jnp.int32)],
        compiler_params=params(10),
        cost_estimate=free(),
        name="query_term",
    )(member, owner, entries, z, w, lse, pos, dep, *([old] if part else []))


def small(kernel, inputs, n_deps, outs, name, aliases=None, flops=0):
    n_vmem = len(inputs) - n_deps
    return pl.pallas_call(
        kernel,
        in_specs=[VMEM] * n_vmem + [ANY] * n_deps,
        out_specs=[VMEM] * len(outs),
        out_shape=[pltpu.VMEM(shape, jnp.float32) for shape in outs],
        input_output_aliases=aliases or {},
        compiler_params=params(4),
        cost_estimate=pl.CostEstimate(flops=flops, bytes_accessed=0, transcendentals=0),
        name=name,
    )(*inputs)


def merge_kernel(*refs):
    xs, out_ref = [r[...] for r in refs[:-1]], refs[-1]
    top = functools.reduce(jnp.maximum, xs)
    out_ref[...] = top + jnp.log(sum(jnp.exp(x - top) for x in xs))


def exchange_lse(lse):
    n = lax.axis_size("cache")
    bits = [1 << i for i in range(n.bit_length() - 1)]
    rounds = [bits[:1]] + [bits[i:i + 2] for i in range(1, len(bits), 2)]
    for some in rounds:
        partners = some if len(some) == 1 else [some[0], some[1], some[0] | some[1]]
        got = [lax.ppermute(lse, "cache", [(i, i ^ p) for i in range(n)]) for p in partners]
        lse = small(merge_kernel, [lse] + got, 0, [lse.shape], "merge_lse")[0]
    return lse


class Line:
    def __init__(self, n, rows, width):
        self.n, self.rows, self.width = n, rows, width
        self.lag_in, self.lag_mid, self.lag_out = LAGS
        self.late = self.lag_in + self.lag_mid
        self.slots = n + self.late + self.lag_out
        self.swap, self.mid, self.inner, self.total = {}, {}, {}, {}
        self.out = None

    def swapped(self, array):
        return lax.ppermute(array, "batch", [(0, 1), (1, 0), (2, 3), (3, 2)])

    def swapped_mid(self, array):
        return lax.ppermute(array, "batch", [(1, 2), (2, 1)])

    def begin(self, a, b, c):
        self.came = [self.swapped(x) for x in (a, b, c)]

    def early(self, a, dep):
        def kernel(own, came, dep, out):
            out[...] = own[...] + came[...]

        self.inner_a = small(kernel, [a, self.came[0], dep], 1, [a.shape], "line_early")[0]
        self.mid_a = self.swapped_mid(self.inner_a)
        return self.inner_a

    def early_more(self, b, rest, dep):
        def kernel(inner, mid, own, came, more, dep, total, away, inner_b):
            at = lax.axis_index("batch")
            total[...] = inner[...] + mid[...]
            away[...] = jnp.where((at == 0) | (at == 3), more[:inner.shape[0], :], total[...])
            inner_b[...] = own[...] + came[...]

        inputs = [self.inner_a, self.mid_a, b, self.came[1], rest, dep]
        self.total_a, away, self.inner_b = small(kernel, inputs, 1, [b.shape] * 3, "line_early_more")
        self.came.append(self.swapped(away))
        self.mid_b = self.swapped_mid(self.inner_b)
        return self.inner_b

    def slot(self, t, chunk, deps):
        n, rows = self.n, self.rows
        u, k, o = t - self.lag_in, t - self.late, t - self.late - self.lag_out
        inputs, plan, outs = [], [], []

        def take(x):
            inputs.append(x)
            return len(inputs) - 1

        def give(shape=(rows, self.width)):
            outs.append(shape)
            return len(outs) - 1

        aliases = {}
        if 0 <= u < n:
            array, first = chunk(u)
            came, row = (self.came[u // 2], u % 2 * rows) if u < 8 else (self.swap[u], 0)
            plan.append(("in", take(array), first, take(came), row, give()))
        if 0 <= k < n:
            pair, row = ((self.inner_b, self.mid_b), k % 2 * rows) if k < 4 else ((self.inner[k], self.mid[k]), 0)
            plan.append(("sum", take(pair[0]), take(pair[1]), row, give()))
        if t < n:
            array, first = chunk(t)
            plan.append(("away", take(array), first, give()))
        if 0 <= o < n:
            pair, row = ((self.total_a, self.came[3]), o * rows) if o < 2 else ((self.total[o], self.swap[o + self.late]), 0)
            args = take(pair[0]), take(pair[1])
            old = None if self.out is None else take(self.out)
            new = give((n * rows, self.width))
            if old is not None:
                aliases = {old: new}
            plan.append(("out",) + args + (new,))
        n_in = len(inputs)
        row_out = row if 0 <= o < 2 else 0

        def kernel(*refs):
            at = lax.axis_index("batch")
            end = (at == 0) | (at == 3)
            res = refs[n_in + len(deps):]
            total = None
            for what, *a in plan:
                if what == "in":
                    res[a[4]][...] = refs[a[0]][a[1]:a[1] + rows, :] + refs[a[2]][a[3]:a[3] + rows, :]
                elif what == "sum":
                    total = refs[a[0]][a[2]:a[2] + rows, :] + refs[a[1]][a[2]:a[2] + rows, :]
                    res[a[3]][...] = total
                elif what == "away":
                    value = refs[a[0]][a[1]:a[1] + rows, :]
                    res[a[2]][...] = value if total is None else jnp.where(end, value, total)
                else:
                    here = slice(row_out, row_out + rows)
                    res[a[2]][o * rows:(o + 1) * rows, :] = jnp.where(end, refs[a[1]][here, :], refs[a[0]][here, :])

        got = small(kernel, inputs + list(deps), len(deps), outs, "line_slot", aliases, SLOT_FLOPS)
        away = None
        for what, *a in plan:
            if what == "in":
                self.inner[u] = got[a[4]]
            elif what == "sum":
                away = self.total[k] = got[a[3]]
            elif what == "away":
                away = got[a[2]]
            else:
                self.out = got[a[2]]
        if away is not None:
            self.swap[t] = self.swapped(away)
        if 0 <= u < n:
            self.mid[u] = self.swapped_mid(self.inner[u])
        return got[0]


class HomeSum:
    def __init__(self, terms):
        self.n = lax.axis_size("cache")
        self.terms = terms
        self.steps, self.rows, self.width = terms.shape[1:]
        self.bits = [1 << i for i in range(1, self.n.bit_length() - 1)]
        self.stage = 0

    def move(self, x, bit):
        return lax.ppermute(x, "cache", [(i, i ^ bit) for i in range(self.n)])

    def start(self, dep):
        def kernel(terms, dep, odd):
            def one(i, _):
                for s in range(odd.shape[1]):
                    odd[i, s] = terms[i, s]
                return 0

            lax.fori_loop(0, odd.shape[0], one, 0)

        odd = small(kernel, [self.terms, dep], 1, [(self.n // 2,) + self.terms.shape[1:]], "home_start")[0]
        self.got = self.move(odd, 1)

    def step(self, dep):
        half = self.rows // 2
        orders = (self.bits, self.bits[::-1])
        last = self.stage == len(self.bits)
        if self.stage == 0:
            inputs = [self.terms, self.got]
            sources = [({2 * i: i for i in range(self.n // 2)}, 0, 1, h * half) for h in (0, 1)]
        else:
            inputs, sources = [], []
            for (place, keep), got in zip(self.kept, self.moved):
                sources.append((place, len(inputs), len(inputs) + 1, 0))
                inputs += [keep, got]
        writes, outs, kept = [], [], []
        for h, (place, a, b, first) in enumerate(sources):
            if last:
                writes.append((h, 0, 0, h * half))
                continue
            bit = orders[h][self.stage]
            far = [r for r in sorted(place) if r & bit]
            near = [r for r in sorted(place) if not r & bit]
            for rs in (far, near):
                outs.append((len(rs), self.steps, half, self.width))
                writes += [(h, r, (len(outs) - 1, i), None) for i, r in enumerate(rs)]
            kept.append({r: i for i, r in enumerate(near)})
        if last:
            outs = [(self.steps, self.rows, self.width)]
        n_in, steps = len(inputs), self.steps
        skip = self.n // 2 if self.stage == 0 else 0

        def kernel(*refs):
            res = refs[n_in + 1:]
            for h, r, to, at in writes:
                place, a, b, first = sources[h]
                i = place[r]

                def one(s, _, a=a, b=b, i=i, first=first, to=to, at=at):
                    value = refs[a][skip + i, s, first:first + half, :] + refs[b][i, s, first:first + half, :]
                    if at is None:
                        res[to[0]][to[1], s] = value
                    else:
                        res[0][s, at:at + half, :] = value
                    return 0

                lax.fori_loop(0, steps, one, 0)

        got = small(kernel, inputs + [dep], 1, outs, "home_sum")
        if last:
            return got[0]
        self.kept = [(kept[h], got[2 * h + 1]) for h in (0, 1)]
        self.moved = [self.move(got[2 * h], orders[h][self.stage]) for h in (0, 1)]
        self.stage += 1
        return got[1]


def on_device(queries, positives, block_list, block_count, refresh_owner, cache, fresh):
    steps, group_rows, width = queries.shape
    groups = group_rows // BLK
    blocks, slab_blocks = cache.shape[0] // BLK, fresh.shape[0] // BLK
    meta = Meta(steps, groups, blocks, slab_blocks)
    me = lax.axis_index("cache")
    block_ids = me * blocks + jnp.arange(blocks, dtype=jnp.int32)
    used = jnp.arange(block_list.shape[2], dtype=jnp.int32)[None, None, :] < block_count[:, :, None]
    ids = jnp.where(used, block_list, -1)
    member = jnp.any(ids[..., None] == block_ids, axis=2)
    member = member.astype(jnp.int32).reshape(meta.rows, blocks)
    owner = refresh_owner.astype(jnp.int32)

    z, w, q, own_lse, entries = run_scores(meta, member, owner, queries, cache, fresh)
    lse = exchange_lse(own_lse)

    half = BLK // 2
    line = Line(2 * blocks, half, width)
    in_line = lax.axis_size("batch") == 4 and blocks > 4
    parts = [1, 1, 1, blocks - 3] if in_line else [blocks]
    grads, dep = [], lse
    for i, part in enumerate(parts):
        grads.append(run_grads(meta, member, z, q, lse, sum(parts[:i]), part, dep))
        dep = grads[-1]
    owners = lax.axis_size("cache")
    share = group_rows // owners
    fast = share == BLK and owners == groups and owners & (owners - 1) == 0 and owners > 2
    home = mine = None

    def chunk(k):
        row = k * half
        for part, grad in zip(parts, grads):
            if row < part * BLK:
                return grad, row
            row -= part * BLK

    if in_line:
        line.begin(*grads[:3])
        dep = line.early(grads[0], grads[3])
    if fast:
        terms = dep = run_terms(meta, member, owner, entries, z, w, lse, positives, True, dep, 0, 2)
    if in_line:
        dep = line.early_more(grads[1], grads[3], dep)
    if fast:
        dep = run_terms(meta, member, owner, entries, z, w, lse, positives, True, dep, 1, 2, terms)
        home = HomeSum(dep)
    if in_line:
        deps = [dep]
        for t in range(8, line.slots):
            deps = [line.slot(t, chunk, deps)]
            if fast and t == START_SLOT:
                home.start(deps[0])
            if fast and t in HOME_SLOTS:
                deps.append(home.step(deps[0]))
                mine = deps[-1]
        grad = line.out
    else:
        grad = lax.psum(grads[0], "batch")
        if fast:
            home.start(lse)
    if fast:
        while home.stage < len(home.bits):
            home.step(lse)
        if mine is None or mine.ndim != 3:
            mine = home.step(lse)
    else:
        term = run_terms(meta, member, owner, entries, z, w, lse, positives, False, lse)
        term = jnp.swapaxes(term, 0, 1).reshape(steps, group_rows, width)
        mine = lax.psum_scatter(term, "cache", scatter_dimension=1, tiled=True)
    return mine, grad


def solution(mesh):
    return jax.shard_map(
        on_device,
        mesh=mesh,
        in_specs=(
            P(None, "batch", None),
            P(None, "batch"),
            P(None, "batch", None),
            P(None, "batch"),
            P(),
            P("cache", None),
            P("cache", None),
        ),
        out_specs=(P(None, ("batch", "cache"), None), P("cache", None)),
        check_vma=False,
    )
```

```python
import functools
import math

import jax
import jax.numpy as jnp
from jax import lax
from jax.experimental import pallas as pl
from jax.experimental.pallas import tpu as pltpu
from jax.sharding import PartitionSpec as P

BLK = 128
LOW = -1e30
LAGS = (4, 2, 2)
HOME_SLOTS = (11, 17, 21)
START_SLOT = 8
SLOT_FLOPS = 3_000_000_000


def dot(a, b, ca, cb):
    return lax.dot_general(a, b, (((ca,), (cb,)), ((), ())), preferred_element_type=jnp.float32)


def split(x):
    hi = x.astype(jnp.bfloat16)
    return hi, (x - hi.astype(jnp.float32)).astype(jnp.bfloat16)


class Meta:
    def __init__(self, steps, groups, blocks, slab_blocks):
        self.steps, self.groups, self.blocks, self.slab_blocks = steps, groups, blocks, slab_blocks
        self.rows = steps * groups
        self.size = self.rows * blocks

    def flags(self, owner, out):
        me = lax.axis_index("cache")
        seen = 0
        for s in range(self.steps):
            own = (owner[s] == me).astype(jnp.int32)
            seen = jnp.maximum(seen, own)
            out[s] = own
            out[self.steps + s] = seen

    def count(self, member, flags, s, sb, j):
        return member[sb, j] + jnp.where(j < self.slab_blocks, flags[s], 0)

    def source(self, flags, s, j):
        return jnp.where((flags[self.steps + s] > 0) & (j < self.slab_blocks), self.blocks + j, j)


def scores_kernel(meta, group, scale, member, owner, q_hbm, cache_hbm, fresh_hbm, z_ref, w_ref, q_ref, lse_ref, entries,
                  cache_ref, fresh_ref, peak, total, flags, pairs, sem):
    copies = [pltpu.make_async_copy(src, dst, sem.at[i]) for i, (src, dst) in enumerate(
        ((cache_hbm, cache_ref), (fresh_hbm, fresh_ref), (q_hbm, q_ref)))]
    for copy in copies:
        copy.start()
    meta.flags(owner, flags)

    def collect(sj, carry):
        n_entries, n_pairs = carry
        s, j = sj // meta.blocks, sj % meta.blocks
        m, held = 0, 0
        for b in range(meta.groups):
            sb = s * meta.groups + b
            on = (meta.count(member, flags, s, sb, j) > 0).astype(jnp.int32)
            pairs[n_pairs] = sb * meta.blocks + j
            n_pairs = n_pairs + on
            held = jnp.where(m % 2 == 0, sb, held)
            entries[n_entries + m // 2] = (held * meta.rows + sb) * meta.blocks + j
            m = m + on

        @pl.when(m % 2 == 1)
        def _():
            entries[n_entries + m // 2] = (held * meta.rows + held) * meta.blocks + j

        return n_entries + (m + 1) // 2, n_pairs

    n_entries, n_pairs = lax.fori_loop(0, meta.steps * meta.blocks, collect, (0, 0))
    for g in range(group):
        entries[n_entries + g] = jnp.where(n_entries > 0, entries[0], 0)
        pairs[n_pairs + g] = 0
    entries[entries.shape[0] - 1] = n_entries
    peak[...] = jnp.full(peak.shape, LOW, jnp.float32)
    total[...] = jnp.zeros(total.shape, jnp.float32)

    for copy, src, at in ((copies[0], cache_ref, 0), (copies[1], fresh_ref, meta.blocks)):
        copy.wait()

        def one(k, _, src=src, at=at):
            hi, lo = split(src[pl.ds(pl.multiple_of(k * BLK, BLK), BLK), :])
            w_ref[at + k, :BLK] = hi
            w_ref[at + k, BLK:] = lo
            return 0

        lax.fori_loop(0, src.shape[0] // BLK, one, 0)
    copies[2].wait()

    def score(it, _):
        found = []
        for g in range(group):
            e = entries[it * group + g]
            j, both = e % meta.blocks, e // meta.blocks
            sb0, sb1 = both // meta.rows, both % meta.rows
            right = jnp.concatenate([q_ref[sb0], q_ref[sb1]], axis=0)
            z = dot(w_ref[meta.source(flags, sb0 // meta.groups, j)], right, 1, 1)
            found.append((sb0, sb1, j, (z[:BLK] + z[BLK:]) * scale))
        for sb0, sb1, j, z in found:
            for sb, one in ((sb0, z[:, :BLK]), (sb1, z[:, BLK:])):
                z_ref[sb, j] = one
                row = pl.ds(sb, 1)
                peak[row, :] = jnp.maximum(peak[row, :], jnp.max(one, axis=0, keepdims=True))
        return 0

    lax.fori_loop(0, (n_entries + group - 1) // group, score, 0)

    def add(it, _):
        found = []
        for g in range(group):
            k = it * group + g
            sb, j = pairs[k] // meta.blocks, pairs[k] % meta.blocks
            c = meta.count(member, flags, sb // meta.groups, sb, j).astype(jnp.float32)
            value = jnp.sum(jnp.exp(z_ref[sb, j] - peak[pl.ds(sb, 1), :]), axis=0, keepdims=True)
            found.append((sb, jnp.where(k < n_pairs, value * c, 0.0)))
        for sb, value in found:
            total[pl.ds(sb, 1), :] += value
        return 0

    lax.fori_loop(0, (n_pairs + group - 1) // group, add, 0)
    sums = total[...]
    lse_ref[...] = jnp.where(sums > 0, peak[...] + jnp.log(jnp.maximum(sums, 1e-30)), LOW)


def grad_kernel(meta, first, width, member, z_ref, q_ref, lse_ref, dep, out_ref, todo):
    def block(i, _):
        j = first + i
        n = 0
        for sb in range(meta.rows):
            todo[n] = sb
            n = n + member[sb, j]
        for g in range(width):
            todo[n + g] = 0
        at = pl.ds(pl.multiple_of(i * BLK, BLK), BLK)
        out_ref[at, :] = jnp.zeros((BLK, out_ref.shape[1]), jnp.float32)

        def step(it, _):
            his, los, rows = [], [], []
            for g in range(width):
                k = it * width + g
                sb = todo[k]
                p = jnp.exp(z_ref[sb, j] - lse_ref[pl.ds(sb, 1), :])
                hi, lo = split(jnp.where(k < n, p, 0.0))
                his.append(hi)
                los.append(lo)
                rows.append(q_ref[sb])
            left = jnp.concatenate([jnp.concatenate(his, axis=1), jnp.concatenate(los, axis=1)], axis=0)
            acc = dot(left, jnp.concatenate(rows, axis=0), 1, 0)
            out_ref[at, :] += acc[:BLK] + acc[BLK:]
            return 0

        lax.fori_loop(0, (n + width - 1) // width, step, 0)
        return 0

    lax.fori_loop(0, out_ref.shape[0] // BLK, block, 0)


def term_kernel(meta, spread, width, part, parts, member, owner, entries, z_ref, w_ref, lse_ref, pos_ref, dep, *refs):
    out_ref, flags, rows_ref = refs[-3:]
    meta.flags(owner, flags)
    me = lax.axis_index("cache")
    below = lax.broadcasted_iota(jnp.int32, (BLK, BLK), 0)
    for s in range(meta.steps):
        for b in range(meta.groups):
            sb = s * meta.groups + b
            rows_ref[sb:sb + 1, :] = pos_ref[s:s + 1, b * BLK:(b + 1) * BLK]

    def clear(i, _):
        for s in range(meta.steps):
            out_ref[i, s] = jnp.zeros(out_ref.shape[2:], jnp.float32)
        return 0

    if part == 0:
        lax.fori_loop(0, meta.groups, clear, 0)
    n = entries[entries.shape[0] - 1]
    trips = (n + width - 1) // width

    def step(it, _):
        found = []
        for g in range(width):
            k = it * width + g
            j, both = entries[k] % meta.blocks, entries[k] // meta.blocks
            sbs = both // meta.rows, both % meta.rows
            s = sbs[0] // meta.groups
            hot = ((flags[s] > 0) & (j < meta.slab_blocks)).astype(jnp.float32)
            his, los = [], []
            for half, sb in enumerate(sbs):
                c = meta.count(member, flags, s, sb, j).astype(jnp.float32)
                p = jnp.exp(z_ref[sb, j] - lse_ref[pl.ds(sb, 1), :]) * c
                row = rows_ref[pl.ds(sb, 1), :] - j * BLK
                p = p - jnp.where(row == below, hot, 0.0)
                live = (k < n) if half == 0 else (k < n) & (sbs[1] != sbs[0])
                hi, lo = split(jnp.where(live, p, 0.0).T)
                his.append(hi)
                los.append(lo)
            hi = jnp.concatenate(his, axis=0)
            w = w_ref[meta.source(flags, s, j)]
            acc = dot(jnp.concatenate([hi, hi], axis=1), w, 1, 0) + dot(jnp.concatenate(los, axis=0), w[:BLK], 1, 0)
            found.append((s, sbs, acc))
        for s, sbs, acc in found:
            for half, sb in enumerate(sbs):
                place = sb - s * meta.groups
                if spread:
                    r = me ^ place
                    place = r // 2 + jnp.where(r % 2 == 1, 0, meta.groups // 2)
                out_ref[place, s] += acc[half * BLK:(half + 1) * BLK]
        return 0

    lax.fori_loop(trips * part // parts, trips * (part + 1) // parts, step, 0)


def params(mib):
    return pltpu.CompilerParams(vmem_limit_bytes=mib * 1024 * 1024)


def free():
    return pl.CostEstimate(flops=0, bytes_accessed=0, transcendentals=0)


SMEM = pl.BlockSpec(memory_space=pltpu.SMEM)
VMEM = pl.BlockSpec(memory_space=pltpu.VMEM)
ANY = pl.BlockSpec(memory_space=pl.ANY)
HBM = pl.BlockSpec(memory_space=pltpu.HBM)


def run_scores(meta, member, owner, queries, cache, fresh):
    width = cache.shape[1]
    group = 6
    n_src = meta.blocks + meta.slab_blocks
    most = meta.steps * meta.blocks * ((meta.groups + 1) // 2)
    return pl.pallas_call(
        functools.partial(scores_kernel, meta, group, 2.0 / math.sqrt(width)),
        in_specs=[SMEM, SMEM, HBM, HBM, HBM],
        out_specs=[VMEM] * 4 + [SMEM],
        out_shape=[
            pltpu.VMEM((meta.rows, meta.blocks, BLK, BLK), jnp.float32),
            pltpu.VMEM((n_src, 2 * BLK, width), jnp.bfloat16),
            pltpu.VMEM((meta.rows, BLK, width), jnp.bfloat16),
            pltpu.VMEM((meta.rows, BLK), jnp.float32),
            jax.ShapeDtypeStruct((most + group + 2,), jnp.int32),
        ],
        scratch_shapes=[
            pltpu.VMEM(cache.shape, jnp.float32),
            pltpu.VMEM(fresh.shape, jnp.float32),
            pltpu.VMEM((meta.rows, BLK), jnp.float32),
            pltpu.VMEM((meta.rows, BLK), jnp.float32),
            pltpu.SMEM((2 * meta.steps,), jnp.int32),
            pltpu.SMEM((meta.size + group,), jnp.int32),
            pltpu.SemaphoreType.DMA((3,)),
        ],
        compiler_params=params(20),
        name="scores",
    )(member, owner, *(pltpu.with_memory_space_constraint(x, pltpu.HBM)
                       for x in (queries.reshape(meta.rows, BLK, width), cache, fresh)))


def run_grads(meta, member, z, q, lse, first, count, dep):
    group = 4
    return pl.pallas_call(
        functools.partial(grad_kernel, meta, first, group),
        in_specs=[SMEM, VMEM, VMEM, VMEM, ANY],
        out_specs=VMEM,
        out_shape=pltpu.VMEM((count * BLK, q.shape[2]), jnp.float32),
        scratch_shapes=[pltpu.SMEM((meta.rows + group,), jnp.int32)],
        compiler_params=params(10),
        cost_estimate=free(),
        name="cache_grad",
    )(member, z, q, lse, dep)


def run_terms(meta, member, owner, entries, z, w, lse, pos, spread, dep, part=0, parts=1, old=None):
    group = 3
    return pl.pallas_call(
        functools.partial(term_kernel, meta, spread, group, part, parts),
        in_specs=[SMEM, SMEM, SMEM, VMEM, VMEM, VMEM, VMEM, ANY] + [VMEM] * (part > 0),
        input_output_aliases={8: 0} if part else {},
        out_specs=VMEM,
        out_shape=pltpu.VMEM((meta.groups, meta.steps, BLK, w.shape[2]), jnp.float32),
        scratch_shapes=[pltpu.SMEM((2 * meta.steps,), jnp.int32), pltpu.VMEM((meta.rows, BLK), jnp.int32)],
        compiler_params=params(10),
        cost_estimate=free(),
        name="query_term",
    )(member, owner, entries, z, w, lse, pos, dep, *([old] if part else []))


def small(kernel, inputs, n_deps, outs, name, aliases=None, flops=0):
    n_vmem = len(inputs) - n_deps
    return pl.pallas_call(
        kernel,
        in_specs=[VMEM] * n_vmem + [ANY] * n_deps,
        out_specs=[VMEM] * len(outs),
        out_shape=[pltpu.VMEM(shape, jnp.float32) for shape in outs],
        input_output_aliases=aliases or {},
        compiler_params=params(4),
        cost_estimate=pl.CostEstimate(flops=flops, bytes_accessed=0, transcendentals=0),
        name=name,
    )(*inputs)


def merge_kernel(*refs):
    xs, out_ref = [r[...] for r in refs[:-1]], refs[-1]
    top = functools.reduce(jnp.maximum, xs)
    out_ref[...] = top + jnp.log(sum(jnp.exp(x - top) for x in xs))


def exchange_lse(lse):
    n = lax.axis_size("cache")
    bits = [1 << i for i in range(n.bit_length() - 1)]
    rounds = [bits[:1]] + [bits[i:i + 2] for i in range(1, len(bits), 2)]
    for some in rounds:
        partners = some if len(some) == 1 else [some[0], some[1], some[0] | some[1]]
        got = [lax.ppermute(lse, "cache", [(i, i ^ p) for i in range(n)]) for p in partners]
        lse = small(merge_kernel, [lse] + got, 0, [lse.shape], "merge_lse")[0]
    return lse


class Line:
    def __init__(self, n, rows, width):
        self.n, self.rows, self.width = n, rows, width
        self.lag_in, self.lag_mid, self.lag_out = LAGS
        self.late = self.lag_in + self.lag_mid
        self.slots = n + self.late + self.lag_out
        self.swap, self.mid, self.inner, self.total = {}, {}, {}, {}
        self.out = None

    def swapped(self, array):
        return lax.ppermute(array, "batch", [(0, 1), (1, 0), (2, 3), (3, 2)])

    def swapped_mid(self, array):
        return lax.ppermute(array, "batch", [(1, 2), (2, 1)])

    def begin(self, a, b, c):
        self.came = [self.swapped(x) for x in (a, b, c)]

    def early(self, a, dep):
        def kernel(own, came, dep, out):
            out[...] = own[...] + came[...]

        self.inner_a = small(kernel, [a, self.came[0], dep], 1, [a.shape], "line_early")[0]
        self.mid_a = self.swapped_mid(self.inner_a)
        return self.inner_a

    def early_more(self, b, rest, dep):
        def kernel(inner, mid, own, came, more, dep, total, away, inner_b):
            at = lax.axis_index("batch")
            total[...] = inner[...] + mid[...]
            away[...] = jnp.where((at == 0) | (at == 3), more[:inner.shape[0], :], total[...])
            inner_b[...] = own[...] + came[...]

        inputs = [self.inner_a, self.mid_a, b, self.came[1], rest, dep]
        self.total_a, away, self.inner_b = small(kernel, inputs, 1, [b.shape] * 3, "line_early_more")
        self.came.append(self.swapped(away))
        self.mid_b = self.swapped_mid(self.inner_b)
        return self.inner_b

    def slot(self, t, chunk, deps):
        n, rows = self.n, self.rows
        u, k, o = t - self.lag_in, t - self.late, t - self.late - self.lag_out
        inputs, plan, outs = [], [], []

        def take(x):
            inputs.append(x)
            return len(inputs) - 1

        def give(shape=(rows, self.width)):
            outs.append(shape)
            return len(outs) - 1

        aliases = {}
        if 0 <= u < n:
            array, first = chunk(u)
            came, row = (self.came[u // 2], u % 2 * rows) if u < 8 else (self.swap[u], 0)
            plan.append(("in", take(array), first, take(came), row, give()))
        if 0 <= k < n:
            pair, row = ((self.inner_b, self.mid_b), k % 2 * rows) if k < 4 else ((self.inner[k], self.mid[k]), 0)
            plan.append(("sum", take(pair[0]), take(pair[1]), row, give()))
        if t < n:
            array, first = chunk(t)
            plan.append(("away", take(array), first, give()))
        if 0 <= o < n:
            pair, row = ((self.total_a, self.came[3]), o * rows) if o < 2 else ((self.total[o], self.swap[o + self.late]), 0)
            args = take(pair[0]), take(pair[1])
            old = None if self.out is None else take(self.out)
            new = give((n * rows, self.width))
            if old is not None:
                aliases = {old: new}
            plan.append(("out",) + args + (new,))
        n_in = len(inputs)
        row_out = row if 0 <= o < 2 else 0

        def kernel(*refs):
            at = lax.axis_index("batch")
            end = (at == 0) | (at == 3)
            res = refs[n_in + len(deps):]
            total = None
            for what, *a in plan:
                if what == "in":
                    res[a[4]][...] = refs[a[0]][a[1]:a[1] + rows, :] + refs[a[2]][a[3]:a[3] + rows, :]
                elif what == "sum":
                    total = refs[a[0]][a[2]:a[2] + rows, :] + refs[a[1]][a[2]:a[2] + rows, :]
                    res[a[3]][...] = total
                elif what == "away":
                    value = refs[a[0]][a[1]:a[1] + rows, :]
                    res[a[2]][...] = value if total is None else jnp.where(end, value, total)
                else:
                    here = slice(row_out, row_out + rows)
                    res[a[2]][o * rows:(o + 1) * rows, :] = jnp.where(end, refs[a[1]][here, :], refs[a[0]][here, :])

        got = small(kernel, inputs + list(deps), len(deps), outs, "line_slot", aliases, SLOT_FLOPS)
        away = None
        for what, *a in plan:
            if what == "in":
                self.inner[u] = got[a[4]]
            elif what == "sum":
                away = self.total[k] = got[a[3]]
            elif what == "away":
                away = got[a[2]]
            else:
                self.out = got[a[2]]
        if away is not None:
            self.swap[t] = self.swapped(away)
        if 0 <= u < n:
            self.mid[u] = self.swapped_mid(self.inner[u])
        return got[0]


class HomeSum:
    def __init__(self, terms):
        self.n = lax.axis_size("cache")
        self.terms = terms
        self.steps, self.rows, self.width = terms.shape[1:]
        self.bits = [1 << i for i in range(1, self.n.bit_length() - 1)]
        self.stage = 0

    def move(self, x, bit):
        return lax.ppermute(x, "cache", [(i, i ^ bit) for i in range(self.n)])

    def start(self, dep):
        def kernel(terms, dep, odd):
            def one(i, _):
                for s in range(odd.shape[1]):
                    odd[i, s] = terms[i, s]
                return 0

            lax.fori_loop(0, odd.shape[0], one, 0)

        odd = small(kernel, [self.terms, dep], 1, [(self.n // 2,) + self.terms.shape[1:]], "home_start")[0]
        self.got = self.move(odd, 1)

    def step(self, dep):
        half = self.rows // 2
        orders = (self.bits, self.bits[::-1])
        last = self.stage == len(self.bits)
        if self.stage == 0:
            inputs = [self.terms, self.got]
            sources = [({2 * i: i for i in range(self.n // 2)}, 0, 1, h * half) for h in (0, 1)]
        else:
            inputs, sources = [], []
            for (place, keep), got in zip(self.kept, self.moved):
                sources.append((place, len(inputs), len(inputs) + 1, 0))
                inputs += [keep, got]
        writes, outs, kept = [], [], []
        for h, (place, a, b, first) in enumerate(sources):
            if last:
                writes.append((h, 0, 0, h * half))
                continue
            bit = orders[h][self.stage]
            far = [r for r in sorted(place) if r & bit]
            near = [r for r in sorted(place) if not r & bit]
            for rs in (far, near):
                outs.append((len(rs), self.steps, half, self.width))
                writes += [(h, r, (len(outs) - 1, i), None) for i, r in enumerate(rs)]
            kept.append({r: i for i, r in enumerate(near)})
        if last:
            outs = [(self.steps, self.rows, self.width)]
        n_in, steps = len(inputs), self.steps
        skip = self.n // 2 if self.stage == 0 else 0

        def kernel(*refs):
            res = refs[n_in + 1:]
            for h, r, to, at in writes:
                place, a, b, first = sources[h]
                i = place[r]

                def one(s, _, a=a, b=b, i=i, first=first, to=to, at=at):
                    value = refs[a][skip + i, s, first:first + half, :] + refs[b][i, s, first:first + half, :]
                    if at is None:
                        res[to[0]][to[1], s] = value
                    else:
                        res[0][s, at:at + half, :] = value
                    return 0

                lax.fori_loop(0, steps, one, 0)

        got = small(kernel, inputs + [dep], 1, outs, "home_sum")
        if last:
            return got[0]
        self.kept = [(kept[h], got[2 * h + 1]) for h in (0, 1)]
        self.moved = [self.move(got[2 * h], orders[h][self.stage]) for h in (0, 1)]
        self.stage += 1
        return got[1]


def on_device(queries, positives, block_list, block_count, refresh_owner, cache, fresh):
    steps, group_rows, width = queries.shape
    groups = group_rows // BLK
    blocks, slab_blocks = cache.shape[0] // BLK, fresh.shape[0] // BLK
    meta = Meta(steps, groups, blocks, slab_blocks)
    me = lax.axis_index("cache")
    block_ids = me * blocks + jnp.arange(blocks, dtype=jnp.int32)
    used = jnp.arange(block_list.shape[2], dtype=jnp.int32)[None, None, :] < block_count[:, :, None]
    ids = jnp.where(used, block_list, -1)
    member = jnp.any(ids[..., None] == block_ids, axis=2)
    member = member.astype(jnp.int32).reshape(meta.rows, blocks)
    owner = refresh_owner.astype(jnp.int32)

    z, w, q, own_lse, entries = run_scores(meta, member, owner, queries, cache, fresh)
    lse = exchange_lse(own_lse)

    half = BLK // 2
    line = Line(2 * blocks, half, width)
    in_line = lax.axis_size("batch") == 4 and blocks > 4
    parts = [1, 1, 1, blocks - 3] if in_line else [blocks]
    grads, dep = [], lse
    for i, part in enumerate(parts):
        grads.append(run_grads(meta, member, z, q, lse, sum(parts[:i]), part, dep))
        dep = grads[-1]
    owners = lax.axis_size("cache")
    share = group_rows // owners
    fast = share == BLK and owners == groups and owners & (owners - 1) == 0 and owners > 2
    home = mine = None

    def chunk(k):
        row = k * half
        for part, grad in zip(parts, grads):
            if row < part * BLK:
                return grad, row
            row -= part * BLK

    if in_line:
        line.begin(*grads[:3])
        dep = line.early(grads[0], grads[3])
    if fast:
        terms = dep = run_terms(meta, member, owner, entries, z, w, lse, positives, True, dep, 0, 2)
    if in_line:
        dep = line.early_more(grads[1], grads[3], dep)
    if fast:
        dep = run_terms(meta, member, owner, entries, z, w, lse, positives, True, dep, 1, 2, terms)
        home = HomeSum(dep)
    if in_line:
        deps = [dep]
        for t in range(8, line.slots):
            deps = [line.slot(t, chunk, deps)]
            if fast and t == START_SLOT:
                home.start(deps[0])
            if fast and t in HOME_SLOTS:
                deps.append(home.step(deps[0]))
                mine = deps[-1]
        grad = line.out
    else:
        grad = lax.psum(grads[0], "batch")
        if fast:
            home.start(lse)
    if fast:
        while home.stage < len(home.bits):
            home.step(lse)
        if mine is None or mine.ndim != 3:
            mine = home.step(lse)
    else:
        term = run_terms(meta, member, owner, entries, z, w, lse, positives, False, lse)
        term = jnp.swapaxes(term, 0, 1).reshape(steps, group_rows, width)
        mine = lax.psum_scatter(term, "cache", scatter_dimension=1, tiled=True)
    return mine, grad


def solution(mesh):
    return jax.shard_map(
        on_device,
        mesh=mesh,
        in_specs=(
            P(None, "batch", None),
            P(None, "batch"),
            P(None, "batch", None),
            P(None, "batch"),
            P(),
            P("cache", None),
            P("cache", None),
        ),
        out_specs=(P(None, ("batch", "cache"), None), P("cache", None)),
        check_vma=False,
    )
```
